512 devices in a mesh: ctx: 64 (over x, z), tp: 8 (over y, core).
Axes of the slice: x: 4, y: 4, z: 16, core: 2. Of those that a mesh axis runs over, the one named last changes fastest.
Arguments:
- queries: bfloat16 [8192, 4096], P(('ctx', 'tp')), may hold values from -8 to 8
- keys: bfloat16 [8192, 1024], P(('ctx', 'tp')), may hold values from -8 to 8
- values: bfloat16 [8192, 1024], P(('ctx', 'tp')), may hold values from -6 to 6
- out_grad: bfloat16 [8192, 4096], P(('ctx', 'tp')), may hold values from -6 to 6
- doc_lengths: int32 [8], replicated, may hold values from 1 to 2048, as said below
- doc_groups: int32 [8], replicated, may hold values from 0 to 1, as said below
Outputs:
- attn_out: bfloat16 [8192, 4096], P('ctx', 'tp')
- grad_q: bfloat16 [8192, 4096], P('ctx', 'tp')
- grad_k: bfloat16 [8192, 1024], P('ctx', 'tp')
- grad_v: bfloat16 [8192, 1024], P('ctx', 'tp')
The draws below stay inside these ranges and needn't reach their ends.
Inputs may be any that keep to these rules, and one draw needn't show every extreme that they name: `doc_lengths`: the documents fill all 8192 tokens. The documents of one group (one value of doc_groups) have lengths that sum to 4096; each group holds 4 documents, exactly one of them of 2048 tokens. `doc_groups`: each group number is named by exactly 4 documents.
All inputs are finite; a program needn't handle non-finite values.
Results may differ from the reference program's by a relative error of at most 0.027.
Values may be sent and summed in bfloat16 or wider, within the bound.
A program may use at most 64 MiB of HBM per device.

```python
import jax
import jax.numpy as jnp
from jax import lax

HD = 128
REP = 4
TOK_DEV = 128
DOCS_G = 4
KV_HEADS = 8
HEADS = 32
GROUP = 32
NGROUP = 2
NDOC = 8
MAXLEN = 2048
TOKENS = 8192


def plan_documents(key):
    plan_key = jax.random.fold_in(key, 71)
    group_keys = jax.random.split(plan_key, NGROUP + 1)

    def one_group(group_key):
        cut_points = jax.random.permutation(group_key, MAXLEN - 1)[:DOCS_G - 2] + 1
        cut_points = jnp.sort(cut_points.astype(jnp.int32))
        bounds = jnp.concatenate([jnp.zeros((1,), jnp.int32), cut_points, jnp.full((1,), MAXLEN, jnp.int32)])
        remaining = bounds[1:] - bounds[:-1]
        return jnp.concatenate([jnp.full((1,), MAXLEN, jnp.int32), remaining])
    lengths_all = jax.vmap(one_group)(group_keys[:NGROUP]).reshape(-1)
    groups_all = jnp.repeat(jnp.arange(NGROUP, dtype=jnp.int32), DOCS_G)
    doc_order = jax.random.permutation(group_keys[NGROUP], NDOC)
    return (lengths_all[doc_order], groups_all[doc_order])


def draw_doc_lengths(key, part):
    lengths, _ = plan_documents(key)
    return lengths


def draw_doc_groups(key, part):
    _, groups = plan_documents(key)
    return groups


def draw_queries(key, part):
    key = jax.random.fold_in(key, 3)
    drawn = jax.random.truncated_normal(key, -6.0, 6.0, (TOKENS, HEADS * HD), jnp.float32)
    return drawn.astype(jnp.bfloat16)


def draw_keys(key, part):
    key = jax.random.fold_in(key, 5)
    drawn = jax.random.truncated_normal(key, -6.0, 6.0, (TOKENS, KV_HEADS * HD), jnp.float32)
    return drawn.astype(jnp.bfloat16)


def block_levels(key, extent, pieces, least, high):
    loudness = 1.0
    for axis_at, parts in pieces:
        heights = jax.random.uniform(jax.random.fold_in(jax.random.fold_in(key, 6), axis_at), (parts,), jnp.float32, least / len(pieces), high / len(pieces))
        loudness = loudness * jnp.repeat(jnp.exp(heights), extent[axis_at] // parts).reshape((-1,) + (1,) * (len(extent) - 1 - axis_at))
    return loudness


def gaussian(stream_key, shape, width, reach, cuts=(), kind=jnp.bfloat16):
    gain = block_levels(stream_key, shape, cuts, -0.22, 0.18) if cuts else 1.0
    values = jax.random.normal(stream_key, shape, jnp.float32) * width * gain
    return jnp.minimum(jnp.maximum(values, -reach), reach).astype(kind)


def setup_inputs(seed: int = 0) -> dict:
    arg_keys = jax.random.split(jax.random.key(seed), 7)
    queries = draw_queries(jax.random.fold_in(arg_keys[6], 71), 0)
    keys = draw_keys(jax.random.fold_in(arg_keys[6], 71), 0)
    values = gaussian(arg_keys[2], (TOKENS, KV_HEADS * HD), 1.0, 6.0, ((0, 512),))
    out_grad = gaussian(arg_keys[3], (TOKENS, HEADS * HD), 1.0, 6.0, ((0, 512),))
    doc_lengths = draw_doc_lengths(jax.random.fold_in(arg_keys[6], 71), 0)
    doc_groups = draw_doc_groups(jax.random.fold_in(arg_keys[6], 71), 0)
    return {"queries": queries, "keys": keys, "values": values, "out_grad": out_grad, "doc_lengths": doc_lengths, "doc_groups": doc_groups}


def doc_tables(doc_lengths, doc_groups):
    doc_ends = jnp.cumsum(doc_lengths).astype(jnp.int32)
    starts = (doc_ends - doc_lengths).astype(jnp.int32)
    doc_order = jnp.arange(doc_lengths.shape[0], dtype=jnp.int32)
    same_group = (doc_groups[:, None] == doc_groups[None, :]) & (doc_order[None, :] < doc_order[:, None])
    offsets = jnp.sum(jnp.where(same_group, doc_lengths[None, :], 0), axis=1).astype(jnp.int32)
    return starts, doc_ends, offsets


def slot_tokens(slot_ids, rows_dev, group_size, doc_lengths, doc_groups, starts, offsets):
    owner_id = slot_ids // rows_dev
    group_rank = (slot_ids % rows_dev) * group_size + owner_id % group_size
    group_id = owner_id // group_size
    matched = (doc_groups[None, :] == group_id[:, None]) & (offsets[None, :] <= group_rank[:, None])
    matched = matched & (group_rank[:, None] < (offsets + doc_lengths)[None, :])
    shift_base = jnp.sum(jnp.where(matched, (starts - offsets)[None, :], 0), axis=1)
    return (shift_base + group_rank).astype(jnp.int32)


def token_fields(tokens, group_size, doc_groups, starts, doc_ends, offsets):
    inside = (starts[None, :] <= tokens[:, None]) & (tokens[:, None] < doc_ends[None, :])
    doc_order = jnp.arange(starts.shape[0], dtype=jnp.int32)
    is_found = jnp.any(inside, axis=1)
    doc_ids = jnp.sum(jnp.where(inside, doc_order[None, :], 0), axis=1).astype(jnp.int32)
    doc_ids = jnp.where(is_found, doc_ids, -1).astype(jnp.int32)
    group_rank = jnp.sum(jnp.where(inside, (offsets - starts)[None, :], 0), axis=1) + tokens
    doc_group = jnp.sum(jnp.where(inside, doc_groups[None, :], 0), axis=1)
    owner_id = doc_group * group_size + group_rank % group_size
    return doc_ids, owner_id.astype(jnp.int32)


def reference(queries, keys, values, out_grad, doc_lengths, doc_groups):
    softmax_scale = HD ** -0.5
    starts, doc_ends, offsets = doc_tables(doc_lengths, doc_groups)
    tokens_all = jnp.arange(TOKENS, dtype=jnp.int32)
    doc_ids, _ = token_fields(tokens_all, GROUP, doc_groups, starts, doc_ends, offsets)
    rows_block = min(128, TOK_DEV)
    blocks = TOKENS // rows_block
    window_rows = rows_block + MAXLEN
    query_four = queries.reshape(TOKENS, KV_HEADS, REP, HD)
    grad_four = out_grad.reshape(TOKENS, KV_HEADS, REP, HD)
    padding = ((MAXLEN, 0), (0, 0), (0, 0))
    key_three = jnp.pad(keys.reshape(TOKENS, KV_HEADS, HD), padding)
    value_three = jnp.pad(values.reshape(TOKENS, KV_HEADS, HD), padding)
    doc_padded = jnp.concatenate([jnp.full((MAXLEN,), -1, jnp.int32), doc_ids])

    def window(number):
        begin_row = (number * rows_block).astype(jnp.int32)
        query_block = lax.dynamic_slice_in_dim(query_four, begin_row, rows_block, 0).astype(jnp.float32)
        grad_block = lax.dynamic_slice_in_dim(grad_four, begin_row, rows_block, 0).astype(jnp.float32)
        key_block = lax.dynamic_slice_in_dim(key_three, begin_row, window_rows, 0).astype(jnp.float32)
        value_block = lax.dynamic_slice_in_dim(value_three, begin_row, window_rows, 0).astype(jnp.float32)
        query_docs = lax.dynamic_slice_in_dim(doc_ids, begin_row, rows_block, 0)
        key_docs = lax.dynamic_slice_in_dim(doc_padded, begin_row, window_rows, 0)
        query_tokens = begin_row + jnp.arange(rows_block, dtype=jnp.int32)
        key_tokens = begin_row - MAXLEN + jnp.arange(window_rows, dtype=jnp.int32)
        allowed = (query_docs[:, None] == key_docs[None, :]) & (key_tokens[None, :] <= query_tokens[:, None])
        scores = jnp.einsum("qgrd,kgd->grqk", query_block, key_block) * softmax_scale
        return query_block, grad_block, key_block, value_block, allowed, scores

    def forward(number):
        _, _, _, value_block, allowed, scores = window(number)
        highest = jnp.max(jnp.where(allowed, scores, -jnp.inf), axis=-1, keepdims=True)
        log_total = highest + jnp.log(jnp.sum(jnp.where(allowed, jnp.exp(scores - highest), 0.0), axis=-1, keepdims=True))
        weights = jnp.where(allowed, jnp.exp(scores - log_total), 0.0).astype(jnp.bfloat16)
        weights = lax.optimization_barrier(weights).astype(jnp.float32)
        output = jnp.einsum("grqk,kgd->qgrd", weights, value_block).astype(jnp.bfloat16)
        return output, log_total

    outputs, log_totals = lax.map(forward, jnp.arange(blocks, dtype=jnp.int32))
    attention = outputs.reshape(TOKENS, KV_HEADS, REP, HD)
    delta = jnp.sum(grad_four.astype(jnp.float32) * attention.astype(jnp.float32), axis=-1)

    def backward(running_state, number):
        key_sums, value_sums = running_state
        query_block, grad_block, key_block, value_block, allowed, scores = window(number)
        begin_row = (number * rows_block).astype(jnp.int32)
        weights = jnp.where(allowed, jnp.exp(scores - log_totals[number]), 0.0)
        rounded = lax.optimization_barrier(weights.astype(jnp.bfloat16)).astype(jnp.float32)
        delta_block = jnp.transpose(lax.dynamic_slice_in_dim(delta, begin_row, rows_block, 0), (1, 2, 0))
        value_terms = jnp.einsum("grqk,qgrd->kgd", rounded, grad_block)
        grad_probs = jnp.einsum("qgrd,kgd->grqk", grad_block, value_block)
        dscore = (weights * (grad_probs - delta_block[..., None])).astype(jnp.bfloat16)
        dscore = lax.optimization_barrier(dscore).astype(jnp.float32)
        query_terms = (jnp.einsum("grqk,kgd->qgrd", dscore, key_block) * softmax_scale).astype(jnp.bfloat16)
        key_terms = jnp.einsum("grqk,qgrd->kgd", dscore, query_block) * softmax_scale
        key_sums = lax.dynamic_update_slice_in_dim(key_sums, lax.dynamic_slice_in_dim(key_sums, begin_row, window_rows, 0) + key_terms, begin_row, 0)
        value_sums = lax.dynamic_update_slice_in_dim(value_sums, lax.dynamic_slice_in_dim(value_sums, begin_row, window_rows, 0) + value_terms, begin_row, 0)
        return (key_sums, value_sums), query_terms

    zeros_kv = jnp.zeros((TOKENS + MAXLEN, KV_HEADS, HD), jnp.float32)
    (key_sums, value_sums), query_grad = lax.scan(backward, (zeros_kv, zeros_kv), jnp.arange(blocks, dtype=jnp.int32))
    held_tokens = slot_tokens(tokens_all, TOK_DEV, GROUP, doc_lengths, doc_groups, starts, offsets)
    attn_out = attention.reshape(TOKENS, HEADS * HD)[held_tokens]
    grad_q = query_grad.reshape(TOKENS, HEADS * HD)[held_tokens]
    grad_k = key_sums[MAXLEN:].reshape(TOKENS, KV_HEADS * HD).astype(jnp.bfloat16)[held_tokens]
    grad_v = value_sums[MAXLEN:].reshape(TOKENS, KV_HEADS * HD).astype(jnp.bfloat16)[held_tokens]
    return attn_out, grad_q, grad_k, grad_v
```

```python
import jax
import jax.numpy as jnp
from jax import lax
from jax.experimental import pallas as pl
from jax.experimental.pallas import tpu as pltpu
from jax.sharding import PartitionSpec as P

HD = 128
REP = 4
BLK = 128
XN = 4
ZN = 16
CTX = XN * ZN
TP = 8
NDOC = 8
HOPS = 8
SCALE = HD ** (-0.5)
SCALE2 = SCALE * 1.4426950408889634
NEG = -1e30
ZR = 48
ZK = 32
MESH = pl.DeviceIdType.MESH
NT = (((1,), (1,)), ((), ()))
NN = (((1,), (0,)), ((), ()))
TN = (((0,), (0,)), ((), ()))
F32 = jnp.float32
BF16 = jnp.bfloat16


def mm(a, b, dims):
    return lax.dot_general(a, b, dims, preferred_element_type=F32)


def lane_iota(width):
    return lax.broadcasted_iota(jnp.int32, (1, width), 1)


def kernel(
    len_ref, grp_ref, q_in, k_in, v_in, g_in,
    o_out, dq_out, dk_out, dv_out,
    qin, gin, kbuf, vbuf, qs, gs, ot, obf, m_ref, l_ref, d_ref, dqt, dqbf, low_ref,
    rs_send, rs_recv, zsend, zrecv, zsend_k, zrecv_k, xsend, xrecv, xsend_k, xrecv_k,
    az, ax, azk, axk, bfin, code_z, code_x, code_zk, code_xk,
    a_ss, a_rs, ag_ss, ag_rs, rs_ss, rs_rs, z_ss, z_rs, x_ss, x_rs, loc_s,
):
    c = lax.axis_index("ctx")
    me = lax.axis_index("tp")
    xi = c // ZN
    zi = c % ZN
    nxt = (c + 1) % CTX
    prv = (c + CTX - 1) % CTX
    up = (c + ZN) % CTX
    down = (c + CTX - ZN) % CTX

    barrier = pltpu.get_barrier_semaphore()

    def greet(ci, pi):
        pl.semaphore_signal(barrier, inc=1, device_id=(ci, pi), device_id_type=MESH)

    @pl.loop(1, TP)
    def _(i):
        greet(c, (me + i) % TP)

    @pl.loop(1, ZN)
    def _(i):
        greet(xi * ZN + (zi + i) % ZN, me)

    @pl.loop(1, XN)
    def _(i):
        greet((xi + i) % XN * ZN + zi, me)

    greet(nxt, me)
    greet(prv, me)
    pl.semaphore_wait(barrier, TP - 1 + ZN - 1 + XN - 1 + 2)

    kinds = (
        (k_in, kbuf.at[0], HD),
        (v_in, vbuf.at[0], HD),
        (q_in, qin, REP * HD),
        (g_in, gin, REP * HD),
    )

    def sent_piece(kind, peer):
        src, dst, width = kinds[kind]
        return pltpu.make_async_remote_copy(
            src_ref=src.at[:, pl.ds(pl.multiple_of(peer * width, width), width)],
            dst_ref=dst.at[pl.ds(pl.multiple_of(me * 16, 16), 16), :],
            send_sem=a_ss.at[kind, peer],
            recv_sem=a_rs.at[kind, me],
            device_id=(c, peer),
            device_id_type=MESH,
        )

    def got_piece(kind, peer):
        src, dst, width = kinds[kind]
        return pltpu.make_async_remote_copy(
            src_ref=src.at[:, pl.ds(pl.multiple_of(peer * width, width), width)],
            dst_ref=dst.at[pl.ds(pl.multiple_of(peer * 16, 16), 16), :],
            send_sem=a_ss.at[kind, peer],
            recv_sem=a_rs.at[kind, peer],
            device_id=(c, peer),
            device_id_type=MESH,
        )

    def own_piece(kind):
        src, dst, width = kinds[kind]
        return pltpu.make_async_copy(
            src.at[:, pl.ds(pl.multiple_of(me * width, width), width)],
            dst.at[pl.ds(pl.multiple_of(me * 16, 16), 16), :],
            loc_s.at[kind],
        )

    for kind in range(4):

        @pl.loop(1, TP)
        def _(i, kind=kind):
            sent_piece(kind, (me + i) % TP).start()

        own_piece(kind).start()

    lens = [len_ref[d] for d in range(NDOC)]
    first = [1 - grp_ref[d] for d in range(NDOC)]
    starts = []
    total = jnp.int32(0)
    for d in range(NDOC):
        starts.append(total)
        total = total + lens[d]

    def count0(position):
        acc = 0
        for d in range(NDOC):
            acc = acc + first[d] * jnp.minimum(jnp.maximum(position - starts[d], 0), lens[d])
        return acc

    base = c * BLK
    jl = lane_iota(REP * BLK)
    tok = base + (jl & (BLK - 1))
    low = jnp.zeros_like(tok)
    for d in range(NDOC):
        low = jnp.maximum(low, jnp.where(tok >= starts[d], starts[d], 0))
    low_ref[...] = low - base

    r0 = count0(base)
    c0 = (count0(base + BLK) - r0 + 15) >> 4
    r1 = base - r0
    before = count0(tok)
    is0 = count0(tok + 1) - before == 1
    rank = jnp.where(is0, before, tok - before)
    k = jnp.where(is0, (rank - r0) >> 4, c0 + ((rank - r1) >> 4))
    zd = rank & (ZN - 1)
    code_z[...] = zd * ZR + k * REP + (jl >> 7)
    half = slice(0, 2 * BLK)
    code_zk[...] = zd[:, half] * ZK + k[:, half] + 9 * (jl[:, half] >> 7)

    row0 = count0(xi * (ZN * BLK))
    row1 = xi * (ZN * BLK) - row0

    def arrived(zs, k):
        begin = (xi * ZN + zs) * BLK
        r0 = count0(begin)
        r0e = count0(begin + BLK)
        r1 = begin - r0
        r1e = begin + BLK - r0e
        c0 = (r0e - r0 + 15) >> 4
        g0 = k < c0
        kk = jnp.where(g0, k, k - c0)
        rb = jnp.where(g0, r0, r1)
        re = jnp.where(g0, r0e, r1e)
        rank = rb + ((zi - rb) & (ZN - 1)) + ZN * kk
        xd = jnp.where(g0, 0, 2) + ((rank >> 4) & 1)
        q = (rank - jnp.where(g0, row0, row1)) >> 5
        return rank < re, xd, q

    jx = lane_iota(ZN * ZR)
    zs = (jx * 43691) >> 21
    rem = jx - ZR * zs
    ok, xd, q = arrived(zs, rem >> 2)
    code_x[...] = jnp.where(ok, xd * 256 + (rem & 3) * 64 + q, -1)
    jk = lane_iota(ZN * ZK)
    e = jk & (ZK - 1)
    kv = jnp.where(e >= 9, 1, 0)
    ok, xd, q = arrived(jk >> 5, e - 9 * kv)
    code_xk[...] = jnp.where(ok, xd * 128 + kv * 64 + q, -1)

    jf = lane_iota(4 * 64)
    xs = jf >> 6
    g1 = xi // 2
    res = (xi % 2) * ZN + zi
    rs0 = count0(xs * (ZN * BLK))
    rs0e = count0((xs + 1) * (ZN * BLK))
    rsb = jnp.where(g1 == 1, xs * (ZN * BLK) - rs0, rs0)
    rse = jnp.where(g1 == 1, (xs + 1) * (ZN * BLK) - rs0e, rs0e)
    rank = rsb + ((res - rsb) & 31) + 32 * (jf & 63)
    code = jnp.where(rank < rse, rank >> 5, -1)
    bfin[...] = jnp.where(
        lax.broadcasted_iota(jnp.int32, (BLK, 256), 0) == code, 1.0, 0.0
    ).astype(BF16)

    def onehot(dst, code, rows, step):
        begin = pl.multiple_of(step * rows, rows)
        ids = begin + lax.broadcasted_iota(jnp.int32, (rows, dst.shape[1]), 0)
        dst[pl.ds(begin, rows), :] = jnp.where(ids == code[...], 1.0, 0.0).astype(BF16)

    def chain(buf, which, src_pos, dst_pos, to):
        return pltpu.make_async_remote_copy(
            src_ref=buf.at[src_pos],
            dst_ref=buf.at[dst_pos],
            send_sem=ag_ss.at[dst_pos, which],
            recv_sem=ag_rs.at[dst_pos, which],
            device_id=(to, me),
            device_id_type=MESH,
        )

    def take(kind):
        @pl.loop(1, TP)
        def _(i):
            got_piece(kind, (me + i) % TP).wait_recv()

        own_piece(kind).wait()

    for which, buf in ((0, kbuf), (1, vbuf)):
        take(which)
        chain(buf, which, 0, 1, nxt).start()
        chain(buf, which, 0, 2, up).start()

    take(2)
    for h in range(REP):
        qs[h * BLK : (h + 1) * BLK, :] = qin[:, h * HD : (h + 1) * HD]

    heads = [slice(h * BLK, (h + 1) * BLK) for h in range(REP)]
    key_row = lax.broadcasted_iota(jnp.int32, (BLK, BLK), 0)
    query_col = lax.broadcasted_iota(jnp.int32, (BLK, BLK), 1)

    def diag_scores(hs):
        raw = mm(kbuf[0], qs[hs, :], NT) * SCALE2
        return jnp.where((key_row <= query_col) & (key_row >= low_ref[:, hs]), raw, NEG)

    for hs in heads:
        s2 = diag_scores(hs)
        m = jnp.max(s2, axis=0, keepdims=True)
        p = jnp.exp2(s2 - m)
        m_ref[:, hs] = m
        l_ref[:, hs] = jnp.sum(p, axis=0, keepdims=True)
        ot[:, hs] = mm(vbuf[0], p.astype(BF16), TN)

    def pair_shift(s):
        rows = lax.broadcasted_iota(jnp.int32, (2 * BLK, BLK), 0)
        return jnp.where(rows < BLK, rows - BLK * s, rows - BLK - BLK * (2 * HOPS + 1 - s))

    def pair(buf, s):
        return buf[pl.ds(2 * s - 1, 2)].reshape(2 * BLK, HD)

    def pair_scores(keys, hs, shift):
        raw = mm(keys, qs[hs, :], NT) * SCALE2
        return jnp.where(shift >= low_ref[:, hs], raw, NEG)

    @pl.loop(1, HOPS + 1)
    def _(s):
        for which, buf in ((0, kbuf), (1, vbuf)):
            chain(buf, which, 0, 2 * s - 1, nxt).wait_recv()
            chain(buf, which, 0, 2 * s, prv).wait_recv()

            @pl.when(s < HOPS)
            def _(which=which, buf=buf):
                chain(buf, which, 2 * s - 1, 2 * s + 1, nxt).start()
                chain(buf, which, 2 * s, 2 * s + 2, prv).start()

        onehot(az, code_z, 96, s - 1)
        onehot(ax, code_x, 128, s - 1)
        onehot(azk, code_zk, 64, s - 1)
        onehot(axk, code_xk, 64, s - 1)
        keys = pair(kbuf, s)
        vals = pair(vbuf, s)
        shift = pair_shift(s)
        for hs in heads:
            s2 = pair_scores(keys, hs, shift)
            m_old = m_ref[:, hs]
            m = jnp.maximum(m_old, jnp.max(s2, axis=0, keepdims=True))
            p = jnp.exp2(s2 - m)
            fade = jnp.exp2(m_old - m)
            m_ref[:, hs] = m
            l_ref[:, hs] = l_ref[:, hs] * fade + jnp.sum(p, axis=0, keepdims=True)
            ot[:, hs] = ot[:, hs] * fade + mm(vals, p.astype(BF16), TN)

    take(3)
    for h, hs in enumerate(heads):
        grad = gin[:, h * HD : (h + 1) * HD]
        gs[hs, :] = grad
        mass = l_ref[:, hs]
        att = (ot[:, hs] / mass).astype(BF16)
        obf[:, hs] = att
        d_ref[:, hs] = jnp.sum(att.astype(F32) * grad.astype(F32).T, axis=0, keepdims=True)
        m_ref[:, hs] = m_ref[:, hs] + jnp.log2(mass)

    def z_copy(kind, src_z, dst_z):
        send, recv = ((zsend.at[0], zrecv.at[0]), (zsend.at[1], zrecv.at[1]), (zsend_k, zrecv_k))[kind]
        return pltpu.make_async_remote_copy(
            src_ref=send.at[dst_z],
            dst_ref=recv.at[src_z],
            send_sem=z_ss.at[kind, dst_z],
            recv_sem=z_rs.at[kind, src_z],
            device_id=(xi * ZN + dst_z, me),
            device_id_type=MESH,
        )

    def z_own(kind):
        send, recv = ((zsend.at[0], zrecv.at[0]), (zsend.at[1], zrecv.at[1]), (zsend_k, zrecv_k))[kind]
        return pltpu.make_async_copy(send.at[zi], recv.at[zi], loc_s.at[4 + kind])

    def x_copy(kind, src_x, dst_x):
        send, recv = ((xsend.at[0], xrecv.at[0]), (xsend.at[1], xrecv.at[1]), (xsend_k, xrecv_k))[kind]
        return pltpu.make_async_remote_copy(
            src_ref=send.at[dst_x],
            dst_ref=recv.at[:, src_x],
            send_sem=x_ss.at[kind, dst_x],
            recv_sem=x_rs.at[kind, src_x],
            device_id=(dst_x * ZN + zi, me),
            device_id_type=MESH,
        )

    def x_own(kind):
        send, recv = ((xsend.at[0], xrecv.at[0]), (xsend.at[1], xrecv.at[1]), (xsend_k, xrecv_k))[kind]
        return pltpu.make_async_copy(send.at[xi], recv.at[:, xi], loc_s.at[7 + kind])

    def z_start(kind):
        z_own(kind).start()

        @pl.loop(1, ZN)
        def _(i):
            z_copy(kind, zi, (zi + i) % ZN).start()

    def z_wait(kind):
        z_own(kind).wait()

        @pl.loop(1, ZN)
        def _(i):
            z_copy(kind, (zi + i) % ZN, (zi + i) % ZN).wait_recv()

    def x_start(kind):
        x_own(kind).start()

        @pl.loop(1, XN)
        def _(i):
            x_copy(kind, xi, (xi + i) % XN).start()

    def x_wait(kind):
        x_own(kind).wait()

        @pl.loop(1, XN)
        def _(i):
            x_copy(kind, (xi + i) % XN, (xi + i) % XN).wait_recv()

    def z_fill(kind, src):
        zsend[kind] = mm(az[...], src[...], NT).astype(BF16).reshape(ZN, ZR, HD)
        z_start(kind)

    def x_fill(kind):
        z_wait(kind)
        rows = zrecv[kind].reshape(ZN * ZR, HD)
        xsend[kind] = mm(ax[...], rows, NN).astype(BF16).reshape(XN, REP, 64, HD)
        x_start(kind)

    def finish(kind, out):
        x_wait(kind)
        for h in range(REP):
            out[:, h * HD : (h + 1) * HD] = mm(
                bfin[...], xrecv[kind, h].reshape(256, HD), NN
            ).astype(BF16)

    def back(side, which, s, to):
        return pltpu.make_async_remote_copy(
            src_ref=rs_send.at[s, side, which],
            dst_ref=rs_recv.at[s - 1, side, which],
            send_sem=rs_ss.at[s, side, which],
            recv_sem=rs_rs.at[s - 1, side, which],
            device_id=(to, me),
            device_id_type=MESH,
        )

    def back_wait(side, which, s):
        pltpu.make_async_remote_copy(
            src_ref=rs_send.at[s, side, which],
            dst_ref=rs_recv.at[s, side, which],
            send_sem=rs_ss.at[s, side, which],
            recv_sem=rs_rs.at[s, side, which],
            device_id=(nxt, me),
            device_id_type=MESH,
        ).wait_recv()

    def grads(s2, hs, keys, vals):
        p = jnp.exp2(s2 - m_ref[:, hs])
        dv = mm(p.astype(BF16), gs[hs, :], NN)
        dp = mm(vals, gs[hs, :], NT)
        ds = (p * (dp - d_ref[:, hs])).astype(BF16)
        dk = mm(ds, qs[hs, :], NN)
        return dk, dv, mm(keys, ds, TN)

    dqt[...] = jnp.zeros_like(dqt)

    @pl.loop(0, HOPS)
    def _(i):
        s = HOPS - i
        keys = pair(kbuf, s)
        vals = pair(vbuf, s)
        shift = pair_shift(s)
        dk = jnp.zeros((2 * BLK, HD), F32)
        dv = jnp.zeros((2 * BLK, HD), F32)
        for hs in heads:
            dk_h, dv_h, dq_h = grads(pair_scores(keys, hs, shift), hs, keys, vals)
            dk = dk + dk_h
            dv = dv + dv_h
            dqt[:, hs] += dq_h
        rs_part = (dk.reshape(2, BLK, HD), dv.reshape(2, BLK, HD))

        @pl.when(s == HOPS)
        def _():
            for which in range(2):
                for side in range(2):
                    rs_send[s, side, which] = rs_part[which][side].astype(BF16)

        @pl.when(s < HOPS)
        def _():
            for which in range(2):
                for side in range(2):
                    back_wait(side, which, s)
                    rs_send[s, side, which] = (
                        rs_part[which][side] + rs_recv[s, side, which].astype(F32)
                    ).astype(BF16)

        for which in range(2):
            back(0, which, s, prv).start()
            back(1, which, s, jnp.where(s == 1, down, nxt)).start()

        @pl.when(s == HOPS)
        def _():
            z_fill(0, obf)

        @pl.when(s == 2)
        def _():
            x_fill(0)

    dk = jnp.zeros((BLK, HD), F32)
    dv = jnp.zeros((BLK, HD), F32)
    for hs in heads:
        dk_h, dv_h, dq_h = grads(diag_scores(hs), hs, kbuf[0], vbuf[0])
        dk = dk + dk_h
        dv = dv + dv_h
        dqbf[:, hs] = ((dqt[:, hs] + dq_h) * SCALE).astype(BF16)
    z_fill(1, dqbf)
    for side in range(2):
        for which in range(2):
            back_wait(side, which, 0)
    dk = dk + rs_recv[0, 0, 0].astype(F32) + rs_recv[0, 1, 0].astype(F32)
    dv = dv + rs_recv[0, 0, 1].astype(F32) + rs_recv[0, 1, 1].astype(F32)
    rows = jnp.concatenate([(dk * SCALE).astype(BF16), dv.astype(BF16)], axis=0)
    zsend_k[...] = mm(azk[...], rows, NN).astype(BF16).reshape(ZN, ZK, HD)
    z_start(2)
    x_fill(1)
    z_wait(2)
    rows = zrecv_k[...].reshape(ZN * ZK, HD)
    xsend_k[...] = mm(axk[...], rows, NN).astype(BF16).reshape(XN, 2, 64, HD)
    x_start(2)
    finish(0, o_out)
    finish(1, dq_out)
    x_wait(2)
    dk_out[...] = mm(bfin[...], xrecv_k[0].reshape(256, HD), NN).astype(BF16)
    dv_out[...] = mm(bfin[...], xrecv_k[1].reshape(256, HD), NN).astype(BF16)

    for kind in range(4):

        @pl.loop(1, TP)
        def _(i, kind=kind):
            sent_piece(kind, (me + i) % TP).wait_send()

    @pl.loop(1, 2 * HOPS + 1)
    def _(pos):
        chain(kbuf, 0, 0, pos, nxt).wait_send()
        chain(vbuf, 1, 0, pos, nxt).wait_send()

    @pl.loop(1, HOPS + 1)
    def _(s):
        for side in range(2):
            for which in range(2):
                back(side, which, s, prv).wait_send()

    for kind in range(3):

        @pl.loop(1, ZN)
        def _(i, kind=kind):
            z_copy(kind, zi, (zi + i) % ZN).wait_send()

        @pl.loop(1, XN)
        def _(i, kind=kind):
            x_copy(kind, xi, (xi + i) % XN).wait_send()


def body(queries, keys, values, out_grad, doc_lengths, doc_groups):
    smem = pl.BlockSpec(memory_space=pltpu.SMEM)
    anywhere = pl.BlockSpec(memory_space=pl.ANY)
    vmem = pl.BlockSpec(memory_space=pltpu.VMEM)
    wide = REP * HD
    dma = pltpu.SemaphoreType.DMA
    return pl.pallas_call(
        kernel,
        out_shape=(
            jax.ShapeDtypeStruct((BLK, wide), BF16),
            jax.ShapeDtypeStruct((BLK, wide), BF16),
            jax.ShapeDtypeStruct((BLK, HD), BF16),
            jax.ShapeDtypeStruct((BLK, HD), BF16),
        ),
        in_specs=[smem, smem, anywhere, anywhere, anywhere, anywhere],
        out_specs=(vmem, vmem, vmem, vmem),
        scratch_shapes=[
            pltpu.VMEM((BLK, wide), BF16),
            pltpu.VMEM((BLK, wide), BF16),
            pltpu.VMEM((2 * HOPS + 1, BLK, HD), BF16),
            pltpu.VMEM((2 * HOPS + 1, BLK, HD), BF16),
            pltpu.VMEM((wide, HD), BF16),
            pltpu.VMEM((wide, HD), BF16),
            pltpu.VMEM((HD, wide), F32),
            pltpu.VMEM((HD, wide), BF16),
            pltpu.VMEM((1, wide), F32),
            pltpu.VMEM((1, wide), F32),
            pltpu.VMEM((1, wide), F32),
            pltpu.VMEM((HD, wide), F32),
            pltpu.VMEM((HD, wide), BF16),
            pltpu.VMEM((1, wide), jnp.int32),
            pltpu.VMEM((HOPS + 1, 2, 2, BLK, HD), BF16),
            pltpu.VMEM((HOPS + 1, 2, 2, BLK, HD), BF16),
            pltpu.VMEM((2, ZN, ZR, HD), BF16),
            pltpu.VMEM((2, ZN, ZR, HD), BF16),
            pltpu.VMEM((ZN, ZK, HD), BF16),
            pltpu.VMEM((ZN, ZK, HD), BF16),
            pltpu.VMEM((2, XN, REP, 64, HD), BF16),
            pltpu.VMEM((2, REP, XN, 64, HD), BF16),
            pltpu.VMEM((XN, 2, 64, HD), BF16),
            pltpu.VMEM((2, XN, 64, HD), BF16),
            pltpu.VMEM((ZN * ZR, wide), BF16),
            pltpu.VMEM((XN * 256, ZN * ZR), BF16),
            pltpu.VMEM((ZN * ZK, 2 * BLK), BF16),
            pltpu.VMEM((XN * 128, ZN * ZK), BF16),
            pltpu.VMEM((BLK, 256), BF16),
            pltpu.VMEM((1, wide), jnp.int32),
            pltpu.VMEM((1, ZN * ZR), jnp.int32),
            pltpu.VMEM((1, 2 * BLK), jnp.int32),
            pltpu.VMEM((1, ZN * ZK), jnp.int32),
            dma((4, TP)),
            dma((4, TP)),
            dma((2 * HOPS + 1, 2)),
            dma((2 * HOPS + 1, 2)),
            dma((HOPS + 1, 2, 2)),
            dma((HOPS + 1, 2, 2)),
            dma((3, ZN)),
            dma((3, ZN)),
            dma((3, XN)),
            dma((3, XN)),
            dma((10,)),
        ],
        compiler_params=pltpu.CompilerParams(
            collective_id=0, has_side_effects=True, vmem_limit_bytes=48 * 1024 * 1024
        ),
    )(doc_lengths, doc_groups, queries, keys, values, out_grad)


def solution(mesh):
    rows = P(("ctx", "tp"), None)
    in_specs = (rows, rows, rows, rows, P(), P())
    out_specs = (P("ctx", "tp"),) * 4
    return jax.shard_map(body, mesh=mesh, in_specs=in_specs, out_specs=out_specs, check_vma=False)
```

```python
import jax
import jax.numpy as jnp
from jax import lax
from jax.experimental import pallas as pl
from jax.experimental.pallas import tpu as pltpu
from jax.sharding import PartitionSpec as P

HD = 128
REP = 4
BLK = 128
XN = 4
ZN = 16
CTX = XN * ZN
TP = 8
NDOC = 8
SUPS = 8
SCALE = HD ** (-0.5)
SCALE2 = SCALE * 1.4426950408889634
NEG = -1e30
ZR = 48
ZK = 32
MESH = pl.DeviceIdType.MESH
NT = (((1,), (1,)), ((), ()))
NN = (((1,), (0,)), ((), ()))
TN = (((0,), (0,)), ((), ()))
F32 = jnp.float32
BF16 = jnp.bfloat16


def mm(a, b, dims):
    return lax.dot_general(a, b, dims, preferred_element_type=F32)


def lane_iota(width):
    return lax.broadcasted_iota(jnp.int32, (1, width), 1)


def kernel(
    len_in, grp_in, q_in, k_in, v_in, g_in,
    o_out, dq_out, dk_out, dv_out,
    len_ref, grp_ref, qin, gin, kv, qs, gs, ot, obf, m_ref, l_ref, d_ref, dqt, dqbf, low_ref,
    keep, part, got, rs_send, rs_recv, zsend, zrecv, zsend_k, zrecv_k,
    xsend, xrecv, xsend_k, xrecv_k,
    az, ax, azk, axk, bfin, code_z, code_x, code_zk, code_xk,
    a_ss, a_rs, kv_ss, kv_rs, ag_ss, ag_rs, d_ss, d_rs, p_ss, p_rs, rs_ss, rs_rs,
    z_ss, z_rs, x_ss, x_rs, loc_s,
):
    c = lax.axis_index("ctx")
    me = lax.axis_index("tp")
    xi = c // ZN
    zi = c % ZN
    half = me % 2
    head = zi // 2
    sup = me // 2 * 2 + zi % 2
    row_block = 2 * sup + half
    here = xi * SUPS + sup
    twin = me + 1 - 2 * half

    def place(superblock, kv_head, core):
        j = superblock % SUPS
        return superblock // SUPS * ZN + 2 * kv_head + j % 2, j // 2 * 2 + core

    def ahead(steps):
        return place((here + steps + XN * SUPS) % (XN * SUPS), head, half)

    def input_to(kv_head, core):
        return place(xi * SUPS + zi // 2, kv_head, core)

    def input_from(core, piece):
        return xi * ZN + 2 * sup + core, piece

    def z_from(block):
        return place(xi * SUPS + block // 2, me, block % 2)

    barrier = pltpu.get_barrier_semaphore()

    def greet(ci, pi):
        pl.semaphore_signal(barrier, inc=1, device_id=(ci, pi), device_id_type=MESH)

    @pl.loop(0, TP)
    def _(i):
        for core in range(2):
            greet(*input_to(i, core))
            greet(*input_from(core, i))
        greet(*ahead(i + 1))
        greet(*ahead(-1 - i))

    @pl.loop(0, ZN)
    def _(i):
        greet(xi * ZN + i, head)
        greet(*z_from(i))

    @pl.loop(1, XN)
    def _(i):
        greet((xi + i) % XN * ZN + zi, me)

    greet(c, twin)
    pl.semaphore_wait(barrier, 6 * TP + 2 * ZN + XN - 1 + 1)

    pltpu.make_async_copy(len_in, len_ref, loc_s.at[0]).start()
    pltpu.make_async_copy(grp_in, grp_ref, loc_s.at[1]).start()

    def copy_to(src, dst, send_sem, recv_sem, to):
        return pltpu.make_async_remote_copy(
            src_ref=src,
            dst_ref=dst,
            send_sem=send_sem,
            recv_sem=recv_sem,
            device_id=to,
            device_id_type=MESH,
        )

    def start_to(src, dst, send_sem, recv_sem, to):
        is_self = (to[0] == c) & (to[1] == me)

        @pl.when(jnp.logical_not(is_self))
        def _():
            copy_to(src, dst, send_sem, recv_sem, to).start()

        @pl.when(is_self)
        def _():
            pltpu.make_async_copy(src, dst, recv_sem).start()

    def left(src, dst, send_sem, recv_sem, to):
        @pl.when((to[0] != c) | (to[1] != me))
        def _():
            copy_to(src, dst, send_sem, recv_sem, to).wait_send()

    def landed(dst, recv_sem):
        pltpu.make_async_copy(dst, dst, recv_sem).wait()

    def rows16(start):
        return pl.ds(pl.multiple_of(start, 16), 16)

    def lanes(kv_head, width):
        return pl.ds(pl.multiple_of(kv_head * width, width), width)

    def kv_piece(kind, kv_head, core):
        return (
            (k_in, v_in)[kind].at[:, lanes(kv_head, HD)],
            kv.at[kind, 0, rows16(zi % 2 * BLK + me * 16), :],
            kv_ss.at[kind, core, kv_head],
            kv_rs.at[kind, zi % 2, me],
            input_to(kv_head, core),
        )

    def wide_piece(kind, kv_head):
        return (
            (q_in, g_in)[kind].at[:, lanes(kv_head, REP * HD)],
            (qin, gin)[kind].at[rows16(me * 16), :],
            a_ss.at[kind, kv_head],
            a_rs.at[kind, me],
            input_to(kv_head, zi % 2),
        )

    @pl.loop(0, TP)
    def _(i):
        for kind in range(2):
            for core in range(2):
                start_to(*kv_piece(kind, (head + i) % TP, core))

    for kind in range(2):

        @pl.loop(0, TP)
        def _(i, kind=kind):
            start_to(*wide_piece(kind, (head + i) % TP))

    pltpu.make_async_copy(len_in, len_ref, loc_s.at[0]).wait()
    pltpu.make_async_copy(grp_in, grp_ref, loc_s.at[1]).wait()
    lens = [len_ref[d] for d in range(NDOC)]
    first = [1 - grp_ref[d] for d in range(NDOC)]
    starts = []
    total = jnp.int32(0)
    for d in range(NDOC):
        starts.append(total)
        total = total + lens[d]

    def count0(position):
        acc = 0
        for d in range(NDOC):
            acc = acc + first[d] * jnp.minimum(jnp.maximum(position - starts[d], 0), lens[d])
        return acc

    sbase = here * (2 * BLK)
    base = sbase + half * BLK
    jl = lane_iota(REP * BLK)
    tok = base + (jl & (BLK - 1))
    low = jnp.zeros_like(tok)
    for d in range(NDOC):
        low = jnp.maximum(low, jnp.where(tok >= starts[d], starts[d], 0))
    low_ref[...] = low - sbase

    def slot(tok, begin, size):
        r0 = count0(begin)
        c0 = (count0(begin + size) - r0 + 15) >> 4
        before = count0(tok)
        is0 = count0(tok + 1) - before == 1
        rank = jnp.where(is0, before, tok - before)
        k = jnp.where(is0, (rank - r0) >> 4, c0 + ((rank - begin + r0) >> 4))
        return rank & (ZN - 1), k

    zd, k = slot(tok, base, BLK)
    code_z[...] = zd * ZR + k * REP + (jl >> 7)
    zd, k = slot(sbase + lane_iota(2 * BLK), sbase, 2 * BLK)
    code_zk[...] = zd * ZK + k

    row0 = count0(xi * (ZN * BLK))
    row1 = xi * (ZN * BLK) - row0

    def arrived(number, size, k):
        begin = xi * (ZN * BLK) + number * size
        r0 = count0(begin)
        r0e = count0(begin + size)
        r1 = begin - r0
        r1e = begin + size - r0e
        c0 = (r0e - r0 + 15) >> 4
        g0 = k < c0
        kk = jnp.where(g0, k, k - c0)
        rb = jnp.where(g0, r0, r1)
        re = jnp.where(g0, r0e, r1e)
        rank = rb + ((zi - rb) & (ZN - 1)) + ZN * kk
        xd = jnp.where(g0, 0, 2) + ((rank >> 4) & 1)
        q = (rank - jnp.where(g0, row0, row1)) >> 5
        return rank < re, xd, q

    jx = lane_iota(ZN * ZR)
    zs = (jx * 43691) >> 21
    rem = jx - ZR * zs
    ok, xd, q = arrived(zs, BLK, rem >> 2)
    code_x[...] = jnp.where(ok, xd * 256 + (rem & 3) * 64 + q, -1)
    jk = lane_iota(ZN * ZK)
    ok, xd, q = arrived(jk >> 6, 2 * BLK, jk & (ZK - 1))
    code_xk[...] = jnp.where(ok, xd * 128 + ((jk >> 5) & 1) * 64 + q, -1)

    jf = lane_iota(4 * 64)
    xs = jf >> 6
    g1 = xi // 2
    res = (xi % 2) * ZN + zi
    rs0 = count0(xs * (ZN * BLK))
    rs0e = count0((xs + 1) * (ZN * BLK))
    rsb = jnp.where(g1 == 1, xs * (ZN * BLK) - rs0, rs0)
    rse = jnp.where(g1 == 1, (xs + 1) * (ZN * BLK) - rs0e, rs0e)
    rank = rsb + ((res - rsb) & 31) + 32 * (jf & 63)
    code = jnp.where(rank < rse, rank >> 5, -1)
    bfin[...] = jnp.where(
        lax.broadcasted_iota(jnp.int32, (BLK, 256), 0) == code, 1.0, 0.0
    ).astype(BF16)

    def onehot(dst, code, rows, step):
        begin = pl.multiple_of(step * rows, rows)
        ids = begin + lax.broadcasted_iota(jnp.int32, (rows, dst.shape[1]), 0)
        dst[pl.ds(begin, rows), :] = jnp.where(ids == code[...], 1.0, 0.0).astype(BF16)

    @pl.loop(0, TP)
    def _(i):
        for kind in range(2):
            for core in range(2):
                landed(kv.at[kind, 0, rows16(core * BLK + i * 16), :], kv_rs.at[kind, core, i])

    def gather(r):
        return copy_to(kv.at[half, 0], kv.at[half, r], ag_ss.at[r], ag_rs.at[r], ahead(r))

    def across(r):
        return copy_to(kv.at[half, r], kv.at[half, r], d_ss.at[r], d_rs.at[r], (c, twin))

    def take(r):
        landed(kv.at[half, r], ag_rs.at[r])
        across(r).start()

    @pl.loop(1, SUPS + 1)
    def _(r):
        gather(r).start()

    def wide_landed(kind):
        @pl.loop(0, TP)
        def _(i):
            landed((qin, gin)[kind].at[rows16(i * 16), :], a_rs.at[kind, i])

    wide_landed(0)
    for h in range(REP):
        qs[h * BLK : (h + 1) * BLK, :] = qin[:, h * HD : (h + 1) * HD]

    heads = [slice(h * BLK, (h + 1) * BLK) for h in range(REP)]
    m_ref[...] = jnp.full_like(m_ref, NEG)
    l_ref[...] = jnp.zeros_like(l_ref)
    ot[...] = jnp.zeros_like(ot)

    def scores(r, hs):
        raw = mm(kv[0, r], qs[hs, :], NT) * SCALE2
        place_in = lax.broadcasted_iota(jnp.int32, (2 * BLK, BLK), 0) - 2 * BLK * r
        query = lax.broadcasted_iota(jnp.int32, (2 * BLK, BLK), 1) + half * BLK
        return jnp.where((place_in <= query) & (place_in >= low_ref[:, hs]), raw, NEG)

    def forward(r):
        for hs in heads:
            s2 = scores(r, hs)
            m_old = m_ref[:, hs]
            m = jnp.maximum(m_old, jnp.max(s2, axis=0, keepdims=True))
            p = jnp.exp2(s2 - m)
            fade = jnp.exp2(m_old - m)
            m_ref[:, hs] = m
            l_ref[:, hs] = l_ref[:, hs] * fade + jnp.sum(p, axis=0, keepdims=True)
            ot[:, hs] = ot[:, hs] * fade + mm(kv[1, r], p.astype(BF16), TN)

    def tables(step):
        onehot(az, code_z, 96, step)
        onehot(ax, code_x, 128, step)
        onehot(azk, code_zk, 64, step)
        onehot(axk, code_xk, 64, step)

    forward(0)

    @pl.loop(0, SUPS)
    def _(step):
        tables(step)

    take(1)

    @pl.loop(1, SUPS + 1)
    def _(r):
        @pl.when(r < SUPS)
        def _():
            take(r + 1)

        landed(kv.at[1 - half, r], d_rs.at[r])
        forward(r)

    wide_landed(1)
    for h, hs in enumerate(heads):
        grad = gin[:, h * HD : (h + 1) * HD]
        gs[hs, :] = grad
        mass = l_ref[:, hs]
        att = (ot[:, hs] / mass).astype(BF16)
        obf[:, hs] = att
        d_ref[:, hs] = jnp.sum(att.astype(F32) * grad.astype(F32).T, axis=0, keepdims=True)
        m_ref[:, hs] = m_ref[:, hs] + jnp.log2(mass)

    zbuf = ((zsend.at[0], zrecv.at[0]), (zsend.at[1], zrecv.at[1]), (zsend_k, zrecv_k))
    xbuf = ((xsend.at[0], xrecv.at[0]), (xsend.at[1], xrecv.at[1]), (xsend_k, xrecv_k))

    def z_move(kind, dst_z):
        send, recv = zbuf[kind]
        return (
            send.at[dst_z],
            recv.at[row_block],
            z_ss.at[kind, dst_z],
            z_rs.at[kind, row_block],
            (xi * ZN + dst_z, head),
        )

    def x_move(kind, dst_x):
        send, recv = xbuf[kind]
        return (
            send.at[dst_x],
            recv.at[:, xi],
            x_ss.at[kind, dst_x],
            x_rs.at[kind, xi],
            (dst_x * ZN + zi, me),
        )

    def z_start(kind):
        @pl.loop(0, ZN)
        def _(i):
            start_to(*z_move(kind, (zi + i) % ZN))

    def z_wait(kind):
        @pl.loop(0, ZN)
        def _(i):
            landed(zbuf[kind][1].at[i], z_rs.at[kind, i])

    def x_start(kind):
        @pl.loop(0, XN)
        def _(i):
            start_to(*x_move(kind, (xi + i) % XN))

    def x_wait(kind):
        @pl.loop(0, XN)
        def _(i):
            landed(xbuf[kind][1].at[:, i], x_rs.at[kind, i])

    def z_fill(kind, src):
        zsend[kind] = mm(az[...], src[...], NT).astype(BF16).reshape(ZN, ZR, HD)
        z_start(kind)

    def x_fill(kind):
        z_wait(kind)
        rows = zrecv[kind].reshape(ZN * ZR, HD)
        xsend[kind] = mm(ax[...], rows, NN).astype(BF16).reshape(XN, REP, 64, HD)
        x_start(kind)

    def finish(kind, out):
        x_wait(kind)
        for h in range(REP):
            out[:, h * HD : (h + 1) * HD] = mm(
                bfin[...], xrecv[kind, h].reshape(256, HD), NN
            ).astype(BF16)

    def to_twin(r):
        return copy_to(part.at[r], got.at[r], p_ss.at[r], p_rs.at[r], (c, twin))

    def to_owner(r):
        return copy_to(rs_send.at[r], rs_recv.at[r], rs_ss.at[r], rs_rs.at[r], ahead(-r))

    def both_cores(r):
        landed(got.at[r], p_rs.at[r])
        return keep[r] + got[r].astype(F32)

    dqt[...] = jnp.zeros_like(dqt)

    @pl.loop(0, SUPS + 1)
    def _(i):
        r = SUPS - i
        dk = jnp.zeros((2 * BLK, HD), F32)
        dv = jnp.zeros((2 * BLK, HD), F32)
        for hs in heads:
            p = jnp.exp2(scores(r, hs) - m_ref[:, hs])
            dv = dv + mm(p.astype(BF16), gs[hs, :], NN)
            dp = mm(kv[1, r], gs[hs, :], NT)
            ds = (p * (dp - d_ref[:, hs])).astype(BF16)
            dk = dk + mm(ds, qs[hs, :], NN)
            dqt[:, hs] += mm(kv[0, r], ds, TN)
        keep[r] = jnp.where(half == 0, dk, dv)
        part[r] = jnp.where(half == 0, dv, dk).astype(BF16)
        to_twin(r).start()

        @pl.when(r < SUPS)
        def _():
            rs_send[r + 1] = both_cores(r + 1).astype(BF16)
            to_owner(r + 1).start()

        @pl.when(r == SUPS)
        def _():
            z_fill(0, obf)

    dqbf[...] = (dqt[...] * SCALE).astype(BF16)
    z_fill(1, dqbf)
    x_fill(0)
    terms = both_cores(0)
    for r in range(1, SUPS + 1):
        landed(rs_recv.at[r], rs_rs.at[r])
        terms = terms + rs_recv[r].astype(F32)
    rows = (terms * jnp.where(half == 0, SCALE, 1.0)).astype(BF16)
    zsend_k[...] = mm(azk[...], rows, NN).astype(BF16).reshape(ZN, ZK, HD)
    z_start(2)
    x_fill(1)
    finish(0, o_out)
    z_wait(2)
    rows = zrecv_k[...].reshape(ZN * ZK, HD)
    xsend_k[...] = mm(axk[...], rows, NN).astype(BF16).reshape(XN, 2, 64, HD)
    x_start(2)
    finish(1, dq_out)
    x_wait(2)
    dk_out[...] = mm(bfin[...], xrecv_k[0].reshape(256, HD), NN).astype(BF16)
    dv_out[...] = mm(bfin[...], xrecv_k[1].reshape(256, HD), NN).astype(BF16)

    @pl.loop(0, TP)
    def _(i):
        for kind in range(2):
            left(*wide_piece(kind, i))
            for core in range(2):
                left(*kv_piece(kind, i, core))

    @pl.loop(1, SUPS + 1)
    def _(r):
        gather(r).wait_send()
        across(r).wait_send()
        to_twin(r).wait_send()
        to_owner(r).wait_send()

    to_twin(0).wait_send()
    for kind in range(3):

        @pl.loop(0, ZN)
        def _(i, kind=kind):
            left(*z_move(kind, i))

        @pl.loop(0, XN)
        def _(i, kind=kind):
            left(*x_move(kind, i))


def body(queries, keys, values, out_grad, doc_lengths, doc_groups):
    anywhere = pl.BlockSpec(memory_space=pl.ANY)
    vmem = pl.BlockSpec(memory_space=pltpu.VMEM)
    wide = REP * HD
    dma = pltpu.SemaphoreType.DMA
    return pl.pallas_call(
        kernel,
        out_shape=(
            jax.ShapeDtypeStruct((BLK, wide), BF16),
            jax.ShapeDtypeStruct((BLK, wide), BF16),
            jax.ShapeDtypeStruct((BLK, HD), BF16),
            jax.ShapeDtypeStruct((BLK, HD), BF16),
        ),
        in_specs=[anywhere] * 6,
        out_specs=(vmem, vmem, vmem, vmem),
        scratch_shapes=[
            pltpu.SMEM((NDOC,), jnp.int32),
            pltpu.SMEM((NDOC,), jnp.int32),
            pltpu.VMEM((BLK, wide), BF16),
            pltpu.VMEM((BLK, wide), BF16),
            pltpu.VMEM((2, SUPS + 1, 2 * BLK, HD), BF16),
            pltpu.VMEM((wide, HD), BF16),
            pltpu.VMEM((wide, HD), BF16),
            pltpu.VMEM((HD, wide), F32),
            pltpu.VMEM((HD, wide), BF16),
            pltpu.VMEM((1, wide), F32),
            pltpu.VMEM((1, wide), F32),
            pltpu.VMEM((1, wide), F32),
            pltpu.VMEM((HD, wide), F32),
            pltpu.VMEM((HD, wide), BF16),
            pltpu.VMEM((1, wide), jnp.int32),
            pltpu.VMEM((SUPS + 1, 2 * BLK, HD), F32),
            pltpu.VMEM((SUPS + 1, 2 * BLK, HD), BF16),
            pltpu.VMEM((SUPS + 1, 2 * BLK, HD), BF16),
            pltpu.VMEM((SUPS + 1, 2 * BLK, HD), BF16),
            pltpu.VMEM((SUPS + 1, 2 * BLK, HD), BF16),
            pltpu.VMEM((2, ZN, ZR, HD), BF16),
            pltpu.VMEM((2, ZN, ZR, HD), BF16),
            pltpu.VMEM((ZN, ZK, HD), BF16),
            pltpu.VMEM((ZN, ZK, HD), BF16),
            pltpu.VMEM((2, XN, REP, 64, HD), BF16),
            pltpu.VMEM((2, REP, XN, 64, HD), BF16),
            pltpu.VMEM((XN, 2, 64, HD), BF16),
            pltpu.VMEM((2, XN, 64, HD), BF16),
            pltpu.VMEM((ZN * ZR, wide), BF16),
            pltpu.VMEM((XN * 256, ZN * ZR), BF16),
            pltpu.VMEM((ZN * ZK, 2 * BLK), BF16),
            pltpu.VMEM((XN * 128, ZN * ZK), BF16),
            pltpu.VMEM((BLK, 256), BF16),
            pltpu.VMEM((1, wide), jnp.int32),
            pltpu.VMEM((1, ZN * ZR), jnp.int32),
            pltpu.VMEM((1, 2 * BLK), jnp.int32),
            pltpu.VMEM((1, ZN * ZK), jnp.int32),
            dma((2, TP)),
            dma((2, TP)),
            dma((2, 2, TP)),
            dma((2, 2, TP)),
            dma((SUPS + 1,)),
            dma((SUPS + 1,)),
            dma((SUPS + 1,)),
            dma((SUPS + 1,)),
            dma((SUPS + 1,)),
            dma((SUPS + 1,)),
            dma((SUPS + 1,)),
            dma((SUPS + 1,)),
            dma((3, ZN)),
            dma((3, ZN)),
            dma((3, XN)),
            dma((3, XN)),
            dma((2,)),
        ],
        compiler_params=pltpu.CompilerParams(
            collective_id=0, has_side_effects=True, vmem_limit_bytes=60 * 1024 * 1024
        ),
    )(doc_lengths, doc_groups, queries, keys, values, out_grad)


def solution(mesh):
    rows = P(("ctx", "tp"), None)
    in_specs = (rows, rows, rows, rows, P(), P())
    out_specs = (P("ctx", "tp"),) * 4
    return jax.shard_map(body, mesh=mesh, in_specs=in_specs, out_specs=out_specs, check_vma=False)
```

```python
import jax
import jax.numpy as jnp
from jax import lax
from jax.experimental import pallas as pl
from jax.experimental.pallas import tpu as pltpu
from jax.sharding import PartitionSpec as P

HD = 128
REP = 4
BLK = 128
XN = 4
ZN = 16
CTX = XN * ZN
TP = 8
NDOC = 8
SUPS = 8
SCALE = HD ** (-0.5)
SCALE2 = SCALE * 1.4426950408889634
NEG = -1e30
ZR = 48
ZK = 32
MESH = pl.DeviceIdType.MESH
NT = (((1,), (1,)), ((), ()))
NN = (((1,), (0,)), ((), ()))
TN = (((0,), (0,)), ((), ()))
F32 = jnp.float32
BF16 = jnp.bfloat16


def mm(a, b, dims):
    return lax.dot_general(a, b, dims, preferred_element_type=F32)


def lane_iota(width):
    return lax.broadcasted_iota(jnp.int32, (1, width), 1)


def kernel(
    len_in, grp_in, q_in, k_in, v_in, g_in,
    o_out, dq_out, dk_out, dv_out,
    len_ref, grp_ref, qin, gin, kv, qs, gs, ot, obf, m_ref, l_ref, d_ref, dqt, dqbf, low_ref,
    keep, part, got, rs_send, rs_recv, zsend, zrecv, zsend_k, zrecv_k,
    xsend, xrecv, xsend_k, xrecv_k,
    az, ax, azk, axk, bfin, code_z, code_x, code_zk, code_xk,
    a_ss, a_rs, kv_ss, kv_rs, ag_ss, ag_rs, d_ss, d_rs, p_ss, p_rs, rs_ss, rs_rs,
    z_ss, z_rs, x_ss, x_rs, loc_s,
):
    c = lax.axis_index("ctx")
    me = lax.axis_index("tp")
    xi = c // ZN
    zi = c % ZN
    half = me % 2
    head = zi // 2
    sup = me // 2 * 2 + zi % 2
    row_block = 2 * sup + half
    here = xi * SUPS + sup
    twin = me + 1 - 2 * half

    def place(superblock, kv_head, core):
        j = superblock % SUPS
        return superblock // SUPS * ZN + 2 * kv_head + j % 2, j // 2 * 2 + core

    def ahead(steps):
        return place((here + steps + XN * SUPS) % (XN * SUPS), head, half)

    def input_to(kv_head, core):
        return place(xi * SUPS + zi // 2, kv_head, core)

    def input_from(core, piece):
        return xi * ZN + 2 * sup + core, piece

    def z_from(block):
        return place(xi * SUPS + block // 2, me, block % 2)

    barrier = pltpu.get_barrier_semaphore()

    def greet(ci, pi):
        pl.semaphore_signal(barrier, inc=1, device_id=(ci, pi), device_id_type=MESH)

    @pl.loop(0, TP)
    def _(i):
        for core in range(2):
            greet(*input_to(i, core))
            greet(*input_from(core, i))
        greet(*ahead(i + 1))
        greet(*ahead(-1 - i))

    @pl.loop(0, ZN)
    def _(i):
        greet(xi * ZN + i, head)
        greet(*z_from(i))

    @pl.loop(1, XN)
    def _(i):
        greet((xi + i) % XN * ZN + zi, me)

    greet(c, twin)
    pl.semaphore_wait(barrier, 6 * TP + 2 * ZN + XN - 1 + 1)

    pltpu.make_async_copy(len_in, len_ref, loc_s.at[0]).start()
    pltpu.make_async_copy(grp_in, grp_ref, loc_s.at[1]).start()

    def copy_to(src, dst, send_sem, recv_sem, to):
        return pltpu.make_async_remote_copy(
            src_ref=src,
            dst_ref=dst,
            send_sem=send_sem,
            recv_sem=recv_sem,
            device_id=to,
            device_id_type=MESH,
        )

    def start_to(src, dst, send_sem, recv_sem, to):
        is_self = (to[0] == c) & (to[1] == me)

        @pl.when(jnp.logical_not(is_self))
        def _():
            copy_to(src, dst, send_sem, recv_sem, to).start()

        @pl.when(is_self)
        def _():
            pltpu.make_async_copy(src, dst, recv_sem).start()

    def left(src, dst, send_sem, recv_sem, to):
        @pl.when((to[0] != c) | (to[1] != me))
        def _():
            copy_to(src, dst, send_sem, recv_sem, to).wait_send()

    def landed(dst, recv_sem):
        pltpu.make_async_copy(dst, dst, recv_sem).wait()

    def rows16(start):
        return pl.ds(pl.multiple_of(start, 16), 16)

    def lanes(kv_head, width):
        return pl.ds(pl.multiple_of(kv_head * width, width), width)

    def kv_piece(kind, kv_head):
        return (
            (k_in, v_in)[kind].at[:, lanes(kv_head, HD)],
            kv.at[kind, 0, rows16(zi % 2 * BLK + me * 16), :],
            kv_ss.at[kind, kv_head],
            kv_rs.at[zi % 2, me],
            input_to(kv_head, kind),
        )

    def wide_piece(kind, kv_head):
        return (
            (q_in, g_in)[kind].at[:, lanes(kv_head, REP * HD)],
            (qin, gin)[kind].at[rows16(me * 16), :],
            a_ss.at[kind, kv_head],
            a_rs.at[kind, me],
            input_to(kv_head, zi % 2),
        )

    @pl.loop(0, TP)
    def _(i):
        for kind in range(2):
            start_to(*kv_piece(kind, (head + i) % TP))

    for kind in range(2):

        @pl.loop(0, TP)
        def _(i, kind=kind):
            start_to(*wide_piece(kind, (head + i) % TP))

    pltpu.make_async_copy(len_in, len_ref, loc_s.at[0]).wait()
    pltpu.make_async_copy(grp_in, grp_ref, loc_s.at[1]).wait()
    lens = [len_ref[d] for d in range(NDOC)]
    first = [1 - grp_ref[d] for d in range(NDOC)]
    starts = []
    total = jnp.int32(0)
    for d in range(NDOC):
        starts.append(total)
        total = total + lens[d]

    def count0(position):
        acc = 0
        for d in range(NDOC):
            acc = acc + first[d] * jnp.minimum(jnp.maximum(position - starts[d], 0), lens[d])
        return acc

    sbase = here * (2 * BLK)
    base = sbase + half * BLK
    jl = lane_iota(REP * BLK)
    tok = base + (jl & (BLK - 1))
    low = jnp.zeros_like(tok)
    for d in range(NDOC):
        low = jnp.maximum(low, jnp.where(tok >= starts[d], starts[d], 0))
    low_ref[...] = low - sbase

    def slot(tok, begin, size):
        r0 = count0(begin)
        c0 = (count0(begin + size) - r0 + 15) >> 4
        before = count0(tok)
        is0 = count0(tok + 1) - before == 1
        rank = jnp.where(is0, before, tok - before)
        k = jnp.where(is0, (rank - r0) >> 4, c0 + ((rank - begin + r0) >> 4))
        return rank & (ZN - 1), k

    zd, k = slot(tok, base, BLK)
    code_z[...] = zd * ZR + k * REP + (jl >> 7)
    zd, k = slot(sbase + lane_iota(2 * BLK), sbase, 2 * BLK)
    code_zk[...] = zd * ZK + k

    row0 = count0(xi * (ZN * BLK))
    row1 = xi * (ZN * BLK) - row0

    def arrived(number, size, k):
        begin = xi * (ZN * BLK) + number * size
        r0 = count0(begin)
        r0e = count0(begin + size)
        r1 = begin - r0
        r1e = begin + size - r0e
        c0 = (r0e - r0 + 15) >> 4
        g0 = k < c0
        kk = jnp.where(g0, k, k - c0)
        rb = jnp.where(g0, r0, r1)
        re = jnp.where(g0, r0e, r1e)
        rank = rb + ((zi - rb) & (ZN - 1)) + ZN * kk
        xd = jnp.where(g0, 0, 2) + ((rank >> 4) & 1)
        q = (rank - jnp.where(g0, row0, row1)) >> 5
        return rank < re, xd, q

    jx = lane_iota(ZN * ZR)
    zs = (jx * 43691) >> 21
    rem = jx - ZR * zs
    ok, xd, q = arrived(zs, BLK, rem >> 2)
    code_x[...] = jnp.where(ok, xd * 256 + (rem & 3) * 64 + q, -1)
    jk = lane_iota(ZN * ZK)
    ok, xd, q = arrived(jk >> 6, 2 * BLK, jk & (ZK - 1))
    code_xk[...] = jnp.where(ok, xd * 128 + ((jk >> 5) & 1) * 64 + q, -1)

    jf = lane_iota(4 * 64)
    xs = jf >> 6
    g1 = xi // 2
    res = (xi % 2) * ZN + zi
    rs0 = count0(xs * (ZN * BLK))
    rs0e = count0((xs + 1) * (ZN * BLK))
    rsb = jnp.where(g1 == 1, xs * (ZN * BLK) - rs0, rs0)
    rse = jnp.where(g1 == 1, (xs + 1) * (ZN * BLK) - rs0e, rs0e)
    rank = rsb + ((res - rsb) & 31) + 32 * (jf & 63)
    code = jnp.where(rank < rse, rank >> 5, -1)
    bfin[...] = jnp.where(
        lax.broadcasted_iota(jnp.int32, (BLK, 256), 0) == code, 1.0, 0.0
    ).astype(BF16)

    def onehot(dst, code, rows, step):
        begin = pl.multiple_of(step * rows, rows)
        ids = begin + lax.broadcasted_iota(jnp.int32, (rows, dst.shape[1]), 0)
        dst[pl.ds(begin, rows), :] = jnp.where(ids == code[...], 1.0, 0.0).astype(BF16)

    @pl.loop(0, SUPS)
    def _(step):
        onehot(az, code_z, 96, step)
        onehot(ax, code_x, 128, step)
        onehot(azk, code_zk, 64, step)
        onehot(axk, code_xk, 64, step)

    @pl.loop(0, TP)
    def _(i):
        for core in range(2):
            landed(kv.at[half, 0, rows16(core * BLK + i * 16), :], kv_rs.at[core, i])

    def gather(r):
        return copy_to(kv.at[half, 0], kv.at[half, r], ag_ss.at[r], ag_rs.at[r], ahead(r))

    def across(r):
        return copy_to(kv.at[half, r], kv.at[half, r], d_ss.at[r], d_rs.at[r], (c, twin))

    def take(r):
        landed(kv.at[half, r], ag_rs.at[r])
        across(r).start()

    @pl.loop(1, SUPS + 1)
    def _(r):
        gather(r).start()

    across(0).start()

    def wide_landed(kind):
        @pl.loop(0, TP)
        def _(i):
            landed((qin, gin)[kind].at[rows16(i * 16), :], a_rs.at[kind, i])

    wide_landed(0)
    for h in range(REP):
        qs[h * BLK : (h + 1) * BLK, :] = qin[:, h * HD : (h + 1) * HD]

    heads = [slice(h * BLK, (h + 1) * BLK) for h in range(REP)]
    m_ref[...] = jnp.full_like(m_ref, NEG)
    l_ref[...] = jnp.zeros_like(l_ref)
    ot[...] = jnp.zeros_like(ot)

    def scores(r, hs):
        raw = mm(kv[0, r], qs[hs, :], NT) * SCALE2
        place_in = lax.broadcasted_iota(jnp.int32, (2 * BLK, BLK), 0) - 2 * BLK * r
        query = lax.broadcasted_iota(jnp.int32, (2 * BLK, BLK), 1) + half * BLK
        return jnp.where((place_in <= query) & (place_in >= low_ref[:, hs]), raw, NEG)

    def forward(r):
        for hs in heads:
            s2 = scores(r, hs)
            m_old = m_ref[:, hs]
            m = jnp.maximum(m_old, jnp.max(s2, axis=0, keepdims=True))
            p = jnp.exp2(s2 - m)
            fade = jnp.exp2(m_old - m)
            m_ref[:, hs] = m
            l_ref[:, hs] = l_ref[:, hs] * fade + jnp.sum(p, axis=0, keepdims=True)
            ot[:, hs] = ot[:, hs] * fade + mm(kv[1, r], p.astype(BF16), TN)

    landed(kv.at[1 - half, 0], d_rs.at[0])
    forward(0)
    take(1)

    @pl.loop(1, SUPS + 1)
    def _(r):
        @pl.when(r < SUPS)
        def _():
            take(r + 1)

        landed(kv.at[1 - half, r], d_rs.at[r])
        forward(r)

    wide_landed(1)
    for h, hs in enumerate(heads):
        grad = gin[:, h * HD : (h + 1) * HD]
        gs[hs, :] = grad
        mass = l_ref[:, hs]
        att = (ot[:, hs] / mass).astype(BF16)
        obf[:, hs] = att
        d_ref[:, hs] = jnp.sum(att.astype(F32) * grad.astype(F32).T, axis=0, keepdims=True)
        m_ref[:, hs] = m_ref[:, hs] + jnp.log2(mass)

    zbuf = ((zsend.at[0], zrecv.at[0]), (zsend.at[1], zrecv.at[1]), (zsend_k, zrecv_k))
    xbuf = ((xsend.at[0], xrecv.at[0]), (xsend.at[1], xrecv.at[1]), (xsend_k, xrecv_k))

    def z_move(kind, dst_z):
        send, recv = zbuf[kind]
        return (
            send.at[dst_z],
            recv.at[row_block],
            z_ss.at[kind, dst_z],
            z_rs.at[kind, row_block],
            (xi * ZN + dst_z, head),
        )

    def x_move(kind, dst_x):
        send, recv = xbuf[kind]
        return (
            send.at[dst_x],
            recv.at[:, xi],
            x_ss.at[kind, dst_x],
            x_rs.at[kind, xi],
            (dst_x * ZN + zi, me),
        )

    def z_start(kind):
        @pl.loop(0, ZN)
        def _(i):
            start_to(*z_move(kind, (zi + i) % ZN))

    def z_wait(kind):
        @pl.loop(0, ZN)
        def _(i):
            landed(zbuf[kind][1].at[i], z_rs.at[kind, i])

    def x_start(kind):
        @pl.loop(0, XN)
        def _(i):
            start_to(*x_move(kind, (xi + i) % XN))

    def x_wait(kind):
        @pl.loop(0, XN)
        def _(i):
            landed(xbuf[kind][1].at[:, i], x_rs.at[kind, i])

    def z_fill(kind, src):
        zsend[kind] = mm(az[...], src[...], NT).astype(BF16).reshape(ZN, ZR, HD)
        z_start(kind)

    def x_fill(kind):
        z_wait(kind)
        rows = zrecv[kind].reshape(ZN * ZR, HD)
        xsend[kind] = mm(ax[...], rows, NN).astype(BF16).reshape(XN, REP, 64, HD)
        x_start(kind)

    def finish(kind, out):
        x_wait(kind)
        for h in range(REP):
            out[:, h * HD : (h + 1) * HD] = mm(
                bfin[...], xrecv[kind, h].reshape(256, HD), NN
            ).astype(BF16)

    def to_twin(r):
        return copy_to(part.at[r], got.at[r], p_ss.at[r], p_rs.at[r], (c, twin))

    def to_owner(r):
        return copy_to(rs_send.at[r], rs_recv.at[r], rs_ss.at[r], rs_rs.at[r], ahead(-r))

    def both_cores(r):
        landed(got.at[r], p_rs.at[r])
        return keep[r] + got[r].astype(F32)

    dqt[...] = jnp.zeros_like(dqt)

    @pl.loop(0, SUPS + 1)
    def _(i):
        r = SUPS - i
        dk = jnp.zeros((2 * BLK, HD), F32)
        dv = jnp.zeros((2 * BLK, HD), F32)
        for hs in heads:
            p = jnp.exp2(scores(r, hs) - m_ref[:, hs])
            dv = dv + mm(p.astype(BF16), gs[hs, :], NN)
            dp = mm(kv[1, r], gs[hs, :], NT)
            ds = (p * (dp - d_ref[:, hs])).astype(BF16)
            dk = dk + mm(ds, qs[hs, :], NN)
            dqt[:, hs] += mm(kv[0, r], ds, TN)
        keep[r] = jnp.where(half == 0, dk, dv)
        part[r] = jnp.where(half == 0, dv, dk).astype(BF16)
        to_twin(r).start()

        @pl.when(r < SUPS)
        def _():
            rs_send[r + 1] = both_cores(r + 1).astype(BF16)
            to_owner(r + 1).start()

        @pl.when(r == SUPS)
        def _():
            z_fill(0, obf)

    dqbf[...] = (dqt[...] * SCALE).astype(BF16)
    z_fill(1, dqbf)
    x_fill(0)
    terms = both_cores(0)
    for r in range(1, SUPS + 1):
        landed(rs_recv.at[r], rs_rs.at[r])
        terms = terms + rs_recv[r].astype(F32)
    rows = (terms * jnp.where(half == 0, SCALE, 1.0)).astype(BF16)
    zsend_k[...] = mm(azk[...], rows, NN).astype(BF16).reshape(ZN, ZK, HD)
    z_start(2)
    x_fill(1)
    finish(0, o_out)
    z_wait(2)
    rows = zrecv_k[...].reshape(ZN * ZK, HD)
    xsend_k[...] = mm(axk[...], rows, NN).astype(BF16).reshape(XN, 2, 64, HD)
    x_start(2)
    finish(1, dq_out)
    x_wait(2)
    dk_out[...] = mm(bfin[...], xrecv_k[0].reshape(256, HD), NN).astype(BF16)
    dv_out[...] = mm(bfin[...], xrecv_k[1].reshape(256, HD), NN).astype(BF16)

    @pl.loop(0, TP)
    def _(i):
        for kind in range(2):
            left(*wide_piece(kind, i))
            left(*kv_piece(kind, i))

    @pl.loop(1, SUPS + 1)
    def _(r):
        gather(r).wait_send()
        across(r).wait_send()
        to_twin(r).wait_send()
        to_owner(r).wait_send()

    across(0).wait_send()
    to_twin(0).wait_send()
    for kind in range(3):

        @pl.loop(0, ZN)
        def _(i, kind=kind):
            left(*z_move(kind, i))

        @pl.loop(0, XN)
        def _(i, kind=kind):
            left(*x_move(kind, i))


def body(queries, keys, values, out_grad, doc_lengths, doc_groups):
    anywhere = pl.BlockSpec(memory_space=pl.ANY)
    vmem = pl.BlockSpec(memory_space=pltpu.VMEM)
    wide = REP * HD
    dma = pltpu.SemaphoreType.DMA
    return pl.pallas_call(
        kernel,
        out_shape=(
            jax.ShapeDtypeStruct((BLK, wide), BF16),
            jax.ShapeDtypeStruct((BLK, wide), BF16),
            jax.ShapeDtypeStruct((BLK, HD), BF16),
            jax.ShapeDtypeStruct((BLK, HD), BF16),
        ),
        in_specs=[anywhere] * 6,
        out_specs=(vmem, vmem, vmem, vmem),
        scratch_shapes=[
            pltpu.SMEM((NDOC,), jnp.int32),
            pltpu.SMEM((NDOC,), jnp.int32),
            pltpu.VMEM((BLK, wide), BF16),
            pltpu.VMEM((BLK, wide), BF16),
            pltpu.VMEM((2, SUPS + 1, 2 * BLK, HD), BF16),
            pltpu.VMEM((wide, HD), BF16),
            pltpu.VMEM((wide, HD), BF16),
            pltpu.VMEM((HD, wide), F32),
            pltpu.VMEM((HD, wide), BF16),
            pltpu.VMEM((1, wide), F32),
            pltpu.VMEM((1, wide), F32),
            pltpu.VMEM((1, wide), F32),
            pltpu.VMEM((HD, wide), F32),
            pltpu.VMEM((HD, wide), BF16),
            pltpu.VMEM((1, wide), jnp.int32),
            pltpu.VMEM((SUPS + 1, 2 * BLK, HD), F32),
            pltpu.VMEM((SUPS + 1, 2 * BLK, HD), BF16),
            pltpu.VMEM((SUPS + 1, 2 * BLK, HD), BF16),
            pltpu.VMEM((SUPS + 1, 2 * BLK, HD), BF16),
            pltpu.VMEM((SUPS + 1, 2 * BLK, HD), BF16),
            pltpu.VMEM((2, ZN, ZR, HD), BF16),
            pltpu.VMEM((2, ZN, ZR, HD), BF16),
            pltpu.VMEM((ZN, ZK, HD), BF16),
            pltpu.VMEM((ZN, ZK, HD), BF16),
            pltpu.VMEM((2, XN, REP, 64, HD), BF16),
            pltpu.VMEM((2, REP, XN, 64, HD), BF16),
            pltpu.VMEM((XN, 2, 64, HD), BF16),
            pltpu.VMEM((2, XN, 64, HD), BF16),
            pltpu.VMEM((ZN * ZR, wide), BF16),
            pltpu.VMEM((XN * 256, ZN * ZR), BF16),
            pltpu.VMEM((ZN * ZK, 2 * BLK), BF16),
            pltpu.VMEM((XN * 128, ZN * ZK), BF16),
            pltpu.VMEM((BLK, 256), BF16),
            pltpu.VMEM((1, wide), jnp.int32),
            pltpu.VMEM((1, ZN * ZR), jnp.int32),
            pltpu.VMEM((1, 2 * BLK), jnp.int32),
            pltpu.VMEM((1, ZN * ZK), jnp.int32),
            dma((2, TP)),
            dma((2, TP)),
            dma((2, TP)),
            dma((2, TP)),
            dma((SUPS + 1,)),
            dma((SUPS + 1,)),
            dma((SUPS + 1,)),
            dma((SUPS + 1,)),
            dma((SUPS + 1,)),
            dma((SUPS + 1,)),
            dma((SUPS + 1,)),
            dma((SUPS + 1,)),
            dma((3, ZN)),
            dma((3, ZN)),
            dma((3, XN)),
            dma((3, XN)),
            dma((2,)),
        ],
        compiler_params=pltpu.CompilerParams(
            collective_id=0, has_side_effects=True, vmem_limit_bytes=60 * 1024 * 1024
        ),
    )(doc_lengths, doc_groups, queries, keys, values, out_grad)


def solution(mesh):
    rows = P(("ctx", "tp"), None)
    in_specs = (rows, rows, rows, rows, P(), P())
    out_specs = (P("ctx", "tp"),) * 4
    return jax.shard_map(body, mesh=mesh, in_specs=in_specs, out_specs=out_specs, check_vma=False)
```

```python
import jax
import jax.numpy as jnp
from jax import lax
from jax.experimental import pallas as pl
from jax.experimental.pallas import tpu as pltpu
from jax.sharding import PartitionSpec as P

HD = 128
REP = 4
BLK = 128
XN = 4
ZN = 16
CTX = XN * ZN
TP = 8
NDOC = 8
SUPS = 8
EXTRA = 17
PLANES = 3
SCALE = HD ** (-0.5)
SCALE2 = SCALE * 1.4426950408889634
NEG = -1e30
ZR = 32
ZK = 32
MESH = pl.DeviceIdType.MESH
NT = (((1,), (1,)), ((), ()))
NN = (((1,), (0,)), ((), ()))
TN = (((0,), (0,)), ((), ()))
F32 = jnp.float32
BF16 = jnp.bfloat16


def mm(a, b, dims):
    return lax.dot_general(a, b, dims, preferred_element_type=F32)


def lane_iota(width):
    return lax.broadcasted_iota(jnp.int32, (1, width), 1)


def kernel(
    len_in, grp_in, q_in, k_in, v_in, g_in,
    xrecv, xrecv_k, bfin, code_f,
    len_ref, grp_ref, qin, gin, kv, qs, gs, ot, obf, m_ref, l_ref, d_ref, dqt, dqbf, low_ref,
    keep, part, got, rs_send, rs_recv, zsend, zrecv, zsend_k, zrecv_k,
    xsend, xsend_k,
    az, ax, azk, axk, aze, extra, code_z, code_e, code_x, code_zk, code_xk,
    a_ss, a_rs, kv_ss, kv_rs, ag_ss, ag_rs, d_ss, d_rs, p_ss, p_rs, rs_ss, rs_rs,
    z_ss, z_rs, x_ss, x_rs, loc_s,
):
    c = lax.axis_index("ctx")
    me = lax.axis_index("tp")
    xi = c // ZN
    zi = c % ZN
    half = me % 2
    head = zi // 2
    sup = me // 2 * 2 + zi % 2
    row_block = 2 * sup + half
    here = xi * SUPS + sup
    twin = me + 1 - 2 * half

    def place(superblock, kv_head, core):
        j = superblock % SUPS
        return superblock // SUPS * ZN + 2 * kv_head + j % 2, j // 2 * 2 + core

    def ahead(steps):
        return place((here + steps + XN * SUPS) % (XN * SUPS), head, half)

    def input_to(kv_head, core):
        return place(xi * SUPS + zi // 2, kv_head, core)

    def input_from(core, piece):
        return xi * ZN + 2 * sup + core, piece

    def z_from(block):
        return place(xi * SUPS + block // 2, me, block % 2)

    barrier = pltpu.get_barrier_semaphore()

    def greet(ci, pi):
        pl.semaphore_signal(barrier, inc=1, device_id=(ci, pi), device_id_type=MESH)

    @pl.loop(0, TP)
    def _(i):
        for core in range(2):
            greet(*input_to(i, core))
            greet(*input_from(core, i))
        greet(*ahead(i + 1))
        greet(*ahead(-1 - i))

    @pl.loop(0, ZN)
    def _(i):
        greet(xi * ZN + i, head)
        greet(*z_from(i))

    @pl.loop(1, XN)
    def _(i):
        greet((xi + i) % XN * ZN + zi, me)

    greet(c, twin)
    pl.semaphore_wait(barrier, 6 * TP + 2 * ZN + XN - 1 + 1)

    pltpu.make_async_copy(len_in, len_ref, loc_s.at[0]).start()
    pltpu.make_async_copy(grp_in, grp_ref, loc_s.at[1]).start()

    def copy_to(src, dst, send_sem, recv_sem, to):
        return pltpu.make_async_remote_copy(
            src_ref=src,
            dst_ref=dst,
            send_sem=send_sem,
            recv_sem=recv_sem,
            device_id=to,
            device_id_type=MESH,
        )

    def start_to(src, dst, send_sem, recv_sem, to):
        is_self = (to[0] == c) & (to[1] == me)

        @pl.when(jnp.logical_not(is_self))
        def _():
            copy_to(src, dst, send_sem, recv_sem, to).start()

        @pl.when(is_self)
        def _():
            pltpu.make_async_copy(src, dst, recv_sem).start()

    def left(src, dst, send_sem, recv_sem, to):
        @pl.when((to[0] != c) | (to[1] != me))
        def _():
            copy_to(src, dst, send_sem, recv_sem, to).wait_send()

    def landed(dst, recv_sem):
        pltpu.make_async_copy(dst, dst, recv_sem).wait()

    def far_first(t, size):
        return jnp.where(t % 2 == 1, size // 2 - (t + 1) // 2, size // 2 + t // 2)

    def rows16(start):
        return pl.ds(pl.multiple_of(start, 16), 16)

    def lanes(kv_head, width):
        return pl.ds(pl.multiple_of(kv_head * width, width), width)

    def kv_piece(kind, kv_head):
        return (
            (k_in, v_in)[kind].at[:, lanes(kv_head, HD)],
            kv.at[kind, 0, rows16(zi % 2 * BLK + me * 16), :],
            kv_ss.at[kind, kv_head],
            kv_rs.at[zi % 2, me],
            input_to(kv_head, kind),
        )

    def wide_piece(kind, kv_head):
        return (
            (q_in, g_in)[kind].at[:, lanes(kv_head, REP * HD)],
            (qin, gin)[kind].at[rows16(me * 16), :],
            a_ss.at[kind, kv_head],
            a_rs.at[kind, me],
            input_to(kv_head, zi % 2),
        )

    @pl.loop(0, TP)
    def _(i):
        for kind in range(2):
            start_to(*kv_piece(kind, (head + far_first(i, TP)) % TP))

    for kind in range(2):

        @pl.loop(0, TP)
        def _(i, kind=kind):
            start_to(*wide_piece(kind, (head + far_first(i, TP)) % TP))

    pltpu.make_async_copy(len_in, len_ref, loc_s.at[0]).wait()
    pltpu.make_async_copy(grp_in, grp_ref, loc_s.at[1]).wait()
    lens = [len_ref[d] for d in range(NDOC)]
    first = [1 - grp_ref[d] for d in range(NDOC)]
    starts = []
    total = jnp.int32(0)
    for d in range(NDOC):
        starts.append(total)
        total = total + lens[d]

    def count0(position):
        acc = 0
        for d in range(NDOC):
            acc = acc + first[d] * jnp.minimum(jnp.maximum(position - starts[d], 0), lens[d])
        return acc

    sbase = here * (2 * BLK)
    base = sbase + half * BLK
    jl = lane_iota(REP * BLK)
    tok = base + (jl & (BLK - 1))
    low = jnp.zeros_like(tok)
    for d in range(NDOC):
        low = jnp.maximum(low, jnp.where(tok >= starts[d], starts[d], 0))
    low_ref[...] = low - sbase

    def slot(tok, begin, size):
        r0 = count0(begin)
        c0 = (count0(begin + size) - r0 + 15) >> 4
        before = count0(tok)
        is0 = count0(tok + 1) - before == 1
        rank = jnp.where(is0, before, tok - before)
        k = jnp.where(is0, (rank - r0) >> 4, c0 + ((rank - begin + r0) >> 4))
        return rank & (ZN - 1), k

    zd, k = slot(tok, base, BLK)
    code_z[...] = jnp.where(k < 8, zd * ZR + k * REP + (jl >> 7), -1)
    code_e[...] = jnp.where(k < 8, -REP - 1, zd * ZK + EXTRA + (jl >> 7))
    zd, k = slot(sbase + lane_iota(2 * BLK), sbase, 2 * BLK)
    code_zk[...] = zd * ZK + k

    row0 = count0(xi * (ZN * BLK))
    row1 = xi * (ZN * BLK) - row0

    def arrived(number, size, k):
        begin = xi * (ZN * BLK) + number * size
        r0 = count0(begin)
        r0e = count0(begin + size)
        r1 = begin - r0
        r1e = begin + size - r0e
        c0 = (r0e - r0 + 15) >> 4
        g0 = k < c0
        kk = jnp.where(g0, k, k - c0)
        rb = jnp.where(g0, r0, r1)
        re = jnp.where(g0, r0e, r1e)
        rank = rb + ((zi - rb) & (ZN - 1)) + ZN * kk
        xd = jnp.where(g0, 0, 2) + ((rank >> 4) & 1)
        q = (rank - jnp.where(g0, row0, row1)) >> 5
        return rank < re, xd, q

    jx = lane_iota(ZN * ZR)
    ok, xd, q = arrived(jx >> 5, BLK, (jx & (ZR - 1)) >> 2)
    code_x[...] = jnp.where(ok, xd * 256 + (jx & 3) * 64 + q, -1)
    jk = lane_iota(ZN * ZK)
    ok, xd, q = arrived(jk >> 6, 2 * BLK, jk & (ZK - 1))
    in_pair = jnp.where(ok, xd * 192 + ((jk >> 5) & 1) * 64 + q, -1)
    row = jk & (ZK - 1)
    begin = xi * (ZN * BLK) + (jk >> 5) * BLK
    holder = 0
    for d in range(1, NDOC):
        holder = holder + jnp.where(starts[d] <= begin, 1, 0)
    ok, xd, _ = arrived(jk >> 5, BLK, jnp.full_like(jk, 8))
    ninth = jnp.where(ok & (row < EXTRA + 8), xd * 192 + 128 + holder * 8 + row - EXTRA, -1)
    code_xk[...] = jnp.where(row < EXTRA, in_pair, ninth)

    jf = lane_iota(4 * 64)
    xs = jf >> 6
    g1 = xi // 2
    res = (xi % 2) * ZN + zi
    rs0 = count0(xs * (ZN * BLK))
    rs0e = count0((xs + 1) * (ZN * BLK))
    rsb = jnp.where(g1 == 1, xs * (ZN * BLK) - rs0, rs0)
    rse = jnp.where(g1 == 1, (xs + 1) * (ZN * BLK) - rs0e, rs0e)
    rank = rsb + ((res - rsb) & 31) + 32 * (jf & 63)
    code = jnp.where(rank < rse, rank >> 5, -1)
    bfin[...] = jnp.where(
        lax.broadcasted_iota(jnp.int32, (BLK, 256), 0) == code, 1.0, 0.0
    ).astype(BF16)

    xs = jf >> 6
    holder = (jf >> 3) & 7
    this_start = 0
    next_start = 0
    for d in range(NDOC - 1):
        this_start = this_start + jnp.where(holder == d, starts[d], 0)
        next_start = next_start + jnp.where(holder == d, starts[d + 1], 0)
    begin = ((next_start - 1) >> 7) << 7
    r0 = count0(begin)
    r0e = count0(begin + BLK)
    rank = begin - r0
    rank = rank + ((zi - rank) & (ZN - 1)) + ZN * (8 - ((r0e - r0 + 15) >> 4))
    ok = (holder < NDOC - 1) & (this_start <= begin) & ((begin >> 11) == xs)
    ok = ok & (rank < begin + BLK - r0e) & (2 + ((rank >> 4) & 1) == xi)
    code_f[...] = jnp.where(ok, rank >> 5, -1)

    def onehot(dst, code, rows, step, shift=0):
        begin = pl.multiple_of(step * rows, rows)
        ids = begin - shift + lax.broadcasted_iota(jnp.int32, (rows, dst.shape[1]), 0)
        dst[pl.ds(begin, rows), :] = jnp.where(ids == code[...], 1.0, 0.0).astype(BF16)

    @pl.loop(0, SUPS)
    def _(step):
        onehot(az, code_z, 64, step)
        onehot(aze.at[0], code_e, 64, step)
        onehot(aze.at[1], code_e, 64, step, REP)
        onehot(ax, code_x, 128, step)
        onehot(azk, code_zk, 64, step)
        onehot(axk, code_xk, 96, step)

    @pl.loop(0, TP)
    def _(i):
        for core in range(2):
            landed(kv.at[half, 0, rows16(core * BLK + i * 16), :], kv_rs.at[core, i])

    def gather(r):
        return copy_to(kv.at[half, 0], kv.at[half, r], ag_ss.at[r], ag_rs.at[r], ahead(r))

    def across(r):
        return copy_to(kv.at[half, r], kv.at[half, r], d_ss.at[r], d_rs.at[r], (c, twin))

    def take(r):
        landed(kv.at[half, r], ag_rs.at[r])
        across(r).start()

    def crossing_first(t):
        return t + 1

    def crossing_last(t):
        return jnp.where(t < SUPS // 2, 2 * t + 2, 2 * t + 1 - SUPS)

    @pl.loop(0, SUPS)
    def _(t):
        gather(crossing_first(t)).start()

    across(0).start()

    def wide_landed(kind):
        @pl.loop(0, TP)
        def _(i):
            landed((qin, gin)[kind].at[rows16(i * 16), :], a_rs.at[kind, i])

    wide_landed(0)
    for h in range(REP):
        qs[h * BLK : (h + 1) * BLK, :] = qin[:, h * HD : (h + 1) * HD]

    heads = [slice(h * BLK, (h + 1) * BLK) for h in range(REP)]
    pairs = [slice(h * BLK, (h + 2) * BLK) for h in range(0, REP, 2)]
    m_ref[...] = jnp.full_like(m_ref, NEG)
    l_ref[...] = jnp.zeros_like(l_ref)
    ot[...] = jnp.zeros_like(ot)

    def scores(r, hs):
        raw = mm(kv[0, r], qs[hs, :], NT) * SCALE2
        place_in = lax.broadcasted_iota(jnp.int32, raw.shape, 0) - 2 * BLK * r
        query = (lax.broadcasted_iota(jnp.int32, raw.shape, 1) & (BLK - 1)) + half * BLK
        return jnp.where((place_in <= query) & (place_in >= low_ref[:, hs]), raw, NEG)

    def forward(r):
        for hs in pairs:
            s2 = scores(r, hs)
            m_old = m_ref[:, hs]
            m = jnp.maximum(m_old, jnp.max(s2, axis=0, keepdims=True))
            p = jnp.exp2(s2 - m)
            fade = jnp.exp2(m_old - m)
            m_ref[:, hs] = m
            l_ref[:, hs] = l_ref[:, hs] * fade + jnp.sum(p, axis=0, keepdims=True)
            ot[:, hs] = ot[:, hs] * fade + mm(kv[1, r], p.astype(BF16), TN)

    landed(kv.at[1 - half, 0], d_rs.at[0])
    forward(0)
    take(crossing_last(0))

    @pl.loop(0, SUPS)
    def _(t):
        @pl.when(t < SUPS - 1)
        def _():
            take(crossing_last(t + 1))

        r = crossing_last(t)
        landed(kv.at[1 - half, r], d_rs.at[r])
        forward(r)

    wide_landed(1)
    for h, hs in enumerate(heads):
        grad = gin[:, h * HD : (h + 1) * HD]
        gs[hs, :] = grad
        mass = l_ref[:, hs]
        att = (ot[:, hs] / mass).astype(BF16)
        obf[:, hs] = att
        d_ref[:, hs] = jnp.sum(att.astype(F32) * grad.astype(F32).T, axis=0, keepdims=True)
        m_ref[:, hs] = m_ref[:, hs] + jnp.log2(mass)

    zbuf = ((zsend.at[0], zrecv.at[0]), (zsend.at[1], zrecv.at[1]), (zsend_k, zrecv_k))
    xbuf = ((xsend.at[0], xrecv.at[0]), (xsend.at[1], xrecv.at[1]), (xsend_k, xrecv_k))

    def z_move(kind, dst_z):
        send, recv = zbuf[kind]
        return (
            send.at[dst_z],
            recv.at[row_block],
            z_ss.at[kind, dst_z],
            z_rs.at[kind, row_block],
            (xi * ZN + dst_z, head),
        )

    def x_move(kind, dst_x):
        send, recv = xbuf[kind]
        return (
            send.at[dst_x],
            recv.at[:, xi],
            x_ss.at[kind, dst_x],
            x_rs.at[kind, xi],
            (dst_x * ZN + zi, me),
        )

    def z_start(kind):
        @pl.loop(0, ZN)
        def _(i):
            start_to(*z_move(kind, (zi + far_first(i, ZN)) % ZN))

    def z_wait(kind):
        @pl.loop(0, ZN)
        def _(i):
            landed(zbuf[kind][1].at[i], z_rs.at[kind, i])

    def x_start(kind):
        @pl.loop(0, XN)
        def _(i):
            start_to(*x_move(kind, (xi + i) % XN))

    def x_wait(kind):
        @pl.loop(0, XN)
        def _(i):
            landed(xbuf[kind][1].at[:, i], x_rs.at[kind, i])

    def z_fill(kind, src):
        zsend[kind] = mm(az[...], src[...], NT).astype(BF16).reshape(ZN, ZR, HD)
        z_start(kind)
        extra[kind] = mm(aze[kind], src[...], NT)

    def x_fill(kind):
        z_wait(kind)
        rows = zrecv[kind].reshape(ZN * ZR, HD)
        xsend[kind] = mm(ax[...], rows, NN).astype(BF16).reshape(XN, REP, 64, HD)
        x_start(kind)

    def to_twin(r):
        return copy_to(part.at[r], got.at[r], p_ss.at[r], p_rs.at[r], (c, twin))

    def to_owner(r):
        return copy_to(rs_send.at[r], rs_recv.at[r], rs_ss.at[r], rs_rs.at[r], ahead(-r))

    def both_cores(r):
        landed(got.at[r], p_rs.at[r])
        return keep[r] + got[r].astype(F32)

    dqt[...] = jnp.zeros_like(dqt)
    z_fill(0, obf)

    @pl.loop(0, SUPS + 1)
    def _(i):
        r = jnp.where(i < SUPS, crossing_first(i), 0)
        dk = jnp.zeros((2 * BLK, HD), F32)
        dv = jnp.zeros((2 * BLK, HD), F32)
        for hs in pairs:
            p = jnp.exp2(scores(r, hs) - m_ref[:, hs])
            dv = dv + mm(p.astype(BF16), gs[hs, :], NN)
            dp = mm(kv[1, r], gs[hs, :], NT)
            ds = (p * (dp - d_ref[:, hs])).astype(BF16)
            dk = dk + mm(ds, qs[hs, :], NN)
            dqt[:, hs] += mm(kv[0, r], ds, TN)
        keep[r] = jnp.where(half == 0, dk, dv)
        part[r] = jnp.where(half == 0, dv, dk).astype(BF16)
        to_twin(r).start()

        @pl.when(i > 0)
        def _():
            done = crossing_first(i - 1)
            rs_send[done] = both_cores(done).astype(BF16)
            to_owner(done).start()


    dqbf[...] = (dqt[...] * SCALE).astype(BF16)
    z_fill(1, dqbf)
    x_fill(0)
    terms = both_cores(0)
    for r in range(1, SUPS + 1):
        landed(rs_recv.at[r], rs_rs.at[r])
        terms = terms + rs_recv[r].astype(F32)
    rows = (terms * jnp.where(half == 0, SCALE, 1.0)).astype(BF16)
    last = mm(azk[...], rows, NN) + extra[0] + extra[1]
    zsend_k[...] = last.astype(BF16).reshape(ZN, ZK, HD)
    z_start(2)
    x_fill(1)
    z_wait(2)
    rows = zrecv_k[...].reshape(ZN * ZK, HD)
    xsend_k[...] = mm(axk[...], rows, NN).astype(BF16).reshape(XN, PLANES, 64, HD)
    x_start(2)
    for kind in range(3):
        x_wait(kind)

    @pl.loop(0, TP)
    def _(i):
        for kind in range(2):
            left(*wide_piece(kind, i))
            left(*kv_piece(kind, i))

    @pl.loop(1, SUPS + 1)
    def _(r):
        gather(r).wait_send()
        across(r).wait_send()
        to_twin(r).wait_send()
        to_owner(r).wait_send()

    across(0).wait_send()
    to_twin(0).wait_send()
    for kind in range(3):

        @pl.loop(0, ZN)
        def _(i, kind=kind):
            left(*z_move(kind, i))

        @pl.loop(0, XN)
        def _(i, kind=kind):
            left(*x_move(kind, i))


def settle(
    rows_in, rows_k_in, place_in, code_in,
    o_out, dq_out, dk_out, dv_out,
    rows, rows_k, place, code, sems,
):
    loads = [
        pltpu.make_async_copy(src, dst, sems.at[i])
        for i, (src, dst) in enumerate(
            ((code_in, code), (place_in, place), (rows_k_in, rows_k), (rows_in, rows))
        )
    ]
    for load in loads:
        load.start()
    for load in loads:
        load.wait()
    late = rows_k[2].reshape(256, HD)
    lane = lax.broadcasted_iota(jnp.int32, (BLK, 256), 1) & 7
    found = lax.broadcasted_iota(jnp.int32, (BLK, 256), 0) == code[...]
    for kind, out in ((0, o_out), (1, dq_out)):
        for h in range(REP):
            pick = jnp.where(found & (lane == kind * REP + h), 1.0, 0.0).astype(BF16)
            both = mm(place[...], rows[kind, h].reshape(256, HD), NN) + mm(pick, late, NN)
            out[:, h * HD : (h + 1) * HD] = both.astype(BF16)
    dk_out[...] = mm(place[...], rows_k[0].reshape(256, HD), NN).astype(BF16)
    dv_out[...] = mm(place[...], rows_k[1].reshape(256, HD), NN).astype(BF16)


def body(queries, keys, values, out_grad, doc_lengths, doc_groups):
    anywhere = pl.BlockSpec(memory_space=pl.ANY)
    vmem = pl.BlockSpec(memory_space=pltpu.VMEM)
    wide = REP * HD
    dma = pltpu.SemaphoreType.DMA
    moved = pl.pallas_call(
        kernel,
        out_shape=(
            jax.ShapeDtypeStruct((2, REP, XN, 64, HD), BF16),
            jax.ShapeDtypeStruct((PLANES, XN, 64, HD), BF16),
            jax.ShapeDtypeStruct((BLK, 256), BF16),
            jax.ShapeDtypeStruct((1, 256), jnp.int32),
        ),
        in_specs=[anywhere] * 6,
        out_specs=(anywhere, anywhere, vmem, vmem),
        scratch_shapes=[
            pltpu.SMEM((NDOC,), jnp.int32),
            pltpu.SMEM((NDOC,), jnp.int32),
            pltpu.VMEM((BLK, wide), BF16),
            pltpu.VMEM((BLK, wide), BF16),
            pltpu.VMEM((2, SUPS + 1, 2 * BLK, HD), BF16),
            pltpu.VMEM((wide, HD), BF16),
            pltpu.VMEM((wide, HD), BF16),
            pltpu.VMEM((HD, wide), F32),
            pltpu.VMEM((HD, wide), BF16),
            pltpu.VMEM((1, wide), F32),
            pltpu.VMEM((1, wide), F32),
            pltpu.VMEM((1, wide), F32),
            pltpu.VMEM((HD, wide), F32),
            pltpu.VMEM((HD, wide), BF16),
            pltpu.VMEM((1, wide), jnp.int32),
            pltpu.VMEM((SUPS + 1, 2 * BLK, HD), F32),
            pltpu.VMEM((SUPS + 1, 2 * BLK, HD), BF16),
            pltpu.VMEM((SUPS + 1, 2 * BLK, HD), BF16),
            pltpu.VMEM((SUPS + 1, 2 * BLK, HD), BF16),
            pltpu.VMEM((SUPS + 1, 2 * BLK, HD), BF16),
            pltpu.VMEM((2, ZN, ZR, HD), BF16),
            pltpu.VMEM((2, ZN, ZR, HD), BF16),
            pltpu.VMEM((ZN, ZK, HD), BF16),
            pltpu.VMEM((ZN, ZK, HD), BF16),
            pltpu.VMEM((2, XN, REP, 64, HD), BF16),
            pltpu.VMEM((XN, PLANES, 64, HD), BF16),
            pltpu.VMEM((ZN * ZR, wide), BF16),
            pltpu.VMEM((XN * 256, ZN * ZR), BF16),
            pltpu.VMEM((ZN * ZK, 2 * BLK), BF16),
            pltpu.VMEM((XN * 64 * PLANES, ZN * ZK), BF16),
            pltpu.VMEM((2, ZN * ZK, wide), BF16),
            pltpu.VMEM((2, ZN * ZK, HD), F32),
            pltpu.VMEM((1, wide), jnp.int32),
            pltpu.VMEM((1, wide), jnp.int32),
            pltpu.VMEM((1, ZN * ZR), jnp.int32),
            pltpu.VMEM((1, 2 * BLK), jnp.int32),
            pltpu.VMEM((1, ZN * ZK), jnp.int32),
            dma((2, TP)),
            dma((2, TP)),
            dma((2, TP)),
            dma((2, TP)),
            dma((SUPS + 1,)),
            dma((SUPS + 1,)),
            dma((SUPS + 1,)),
            dma((SUPS + 1,)),
            dma((SUPS + 1,)),
            dma((SUPS + 1,)),
            dma((SUPS + 1,)),
            dma((SUPS + 1,)),
            dma((3, ZN)),
            dma((3, ZN)),
            dma((3, XN)),
            dma((3, XN)),
            dma((2,)),
        ],
        compiler_params=pltpu.CompilerParams(
            collective_id=0, has_side_effects=True, vmem_limit_bytes=60 * 1024 * 1024
        ),
    )(doc_lengths, doc_groups, queries, keys, values, out_grad)
    return pl.pallas_call(
        settle,
        out_shape=(
            jax.ShapeDtypeStruct((BLK, wide), BF16),
            jax.ShapeDtypeStruct((BLK, wide), BF16),
            jax.ShapeDtypeStruct((BLK, HD), BF16),
            jax.ShapeDtypeStruct((BLK, HD), BF16),
        ),
        in_specs=[anywhere] * 4,
        out_specs=(vmem,) * 4,
        scratch_shapes=[
            pltpu.VMEM((2, REP, XN, 64, HD), BF16),
            pltpu.VMEM((PLANES, XN, 64, HD), BF16),
            pltpu.VMEM((BLK, 256), BF16),
            pltpu.VMEM((1, 256), jnp.int32),
            dma((4,)),
        ],
        compiler_params=pltpu.CompilerParams(vmem_limit_bytes=60 * 1024 * 1024),
    )(*moved)


def solution(mesh):
    rows = P(("ctx", "tp"), None)
    in_specs = (rows, rows, rows, rows, P(), P())
    out_specs = (P("ctx", "tp"),) * 4
    return jax.shard_map(body, mesh=mesh, in_specs=in_specs, out_specs=out_specs, check_vma=False)
```

```python
import jax
import jax.numpy as jnp
from jax import lax
from jax.experimental import pallas as pl
from jax.experimental.pallas import tpu as pltpu
from jax.sharding import PartitionSpec as P

HD = 128
REP = 4
BLK = 128
XN = 4
ZN = 16
CTX = XN * ZN
TP = 8
NDOC = 8
SUPS = 8
EXTRA = 17
PLANES = 3
SCALE = HD ** (-0.5)
SCALE2 = SCALE * 1.4426950408889634
NEG = -1e30
ZR = 32
ZK = 32
MESH = pl.DeviceIdType.MESH
NT = (((1,), (1,)), ((), ()))
NN = (((1,), (0,)), ((), ()))
TN = (((0,), (0,)), ((), ()))
F32 = jnp.float32
BF16 = jnp.bfloat16


def mm(a, b, dims):
    return lax.dot_general(a, b, dims, preferred_element_type=F32)


def lane_iota(width):
    return lax.broadcasted_iota(jnp.int32, (1, width), 1)


def kernel(
    len_in, grp_in, q_in, k_in, v_in, g_in,
    xrecv, xrecv_k, bfin, code_f,
    len_ref, grp_ref, qin, gin, kv, qs, gs, ot, obf, m_ref, l_ref, d_ref, dqt, dqbf, low_ref,
    keep, part, got, rs_send, rs_recv, zsend, zrecv, zsend_k, zrecv_k,
    xsend, xsend_k,
    az, ax, azk, axk, aze, extra, code_z, code_e, code_x, code_zk, code_xk,
    a_ss, a_rs, kv_ss, kv_rs, ag_ss, ag_rs, d_ss, d_rs, p_ss, p_rs, rs_ss, rs_rs,
    z_ss, z_rs, x_ss, x_rs, loc_s,
):
    c = lax.axis_index("ctx")
    me = lax.axis_index("tp")
    xi = c // ZN
    zi = c % ZN
    half = me % 2
    head = zi // 2
    sup = me // 2 * 2 + zi % 2
    row_block = 2 * sup + half
    here = xi * SUPS + sup
    twin = me + 1 - 2 * half

    def place(superblock, kv_head, core):
        j = superblock % SUPS
        return superblock // SUPS * ZN + 2 * kv_head + j % 2, j // 2 * 2 + core

    def ahead(steps):
        return place((here + steps + XN * SUPS) % (XN * SUPS), head, half)

    def input_to(kv_head, core):
        return place(xi * SUPS + zi // 2, kv_head, core)

    def input_from(core, piece):
        return xi * ZN + 2 * sup + core, piece

    def z_from(block):
        return place(xi * SUPS + block // 2, me, block % 2)

    barrier = pltpu.get_barrier_semaphore()

    def greet(ci, pi):
        pl.semaphore_signal(barrier, inc=1, device_id=(ci, pi), device_id_type=MESH)

    @pl.loop(0, TP)
    def _(i):
        for core in range(2):
            greet(*input_to(i, core))
            greet(*input_from(core, i))
        greet(*ahead(i + 1))
        greet(*ahead(-1 - i))

    @pl.loop(0, ZN)
    def _(i):
        greet(xi * ZN + i, head)
        greet(*z_from(i))

    @pl.loop(1, XN)
    def _(i):
        greet((xi + i) % XN * ZN + zi, me)

    greet(c, twin)
    pl.semaphore_wait(barrier, 6 * TP + 2 * ZN + XN - 1 + 1)

    pltpu.make_async_copy(len_in, len_ref, loc_s.at[0]).start()
    pltpu.make_async_copy(grp_in, grp_ref, loc_s.at[1]).start()

    def copy_to(src, dst, send_sem, recv_sem, to):
        return pltpu.make_async_remote_copy(
            src_ref=src,
            dst_ref=dst,
            send_sem=send_sem,
            recv_sem=recv_sem,
            device_id=to,
            device_id_type=MESH,
        )

    def start_to(src, dst, send_sem, recv_sem, to):
        is_self = (to[0] == c) & (to[1] == me)

        @pl.when(jnp.logical_not(is_self))
        def _():
            copy_to(src, dst, send_sem, recv_sem, to).start()

        @pl.when(is_self)
        def _():
            pltpu.make_async_copy(src, dst, recv_sem).start()

    def left(src, dst, send_sem, recv_sem, to):
        @pl.when((to[0] != c) | (to[1] != me))
        def _():
            copy_to(src, dst, send_sem, recv_sem, to).wait_send()

    def landed(dst, recv_sem):
        pltpu.make_async_copy(dst, dst, recv_sem).wait()

    def far_first(t, size):
        return jnp.where(t % 2 == 1, size // 2 - (t + 1) // 2, size // 2 + t // 2)

    def rows16(start):
        return pl.ds(pl.multiple_of(start, 16), 16)

    def lanes(kv_head, width):
        return pl.ds(pl.multiple_of(kv_head * width, width), width)

    def kv_piece(kind, kv_head):
        return (
            (k_in, v_in)[kind].at[:, lanes(kv_head, HD)],
            kv.at[kind, 0, rows16(zi % 2 * BLK + me * 16), :],
            kv_ss.at[kind, kv_head],
            kv_rs.at[zi % 2, me],
            input_to(kv_head, kind),
        )

    def wide_piece(kind, kv_head):
        return (
            (q_in, g_in)[kind].at[:, lanes(kv_head, REP * HD)],
            (qin, gin)[kind].at[rows16(me * 16), :],
            a_ss.at[kind, kv_head],
            a_rs.at[kind, me],
            input_to(kv_head, zi % 2),
        )

    @pl.loop(0, TP)
    def _(i):
        for kind in range(2):
            start_to(*kv_piece(kind, (head + far_first(i, TP)) % TP))

    def wide_start(kind):
        @pl.loop(0, TP)
        def _(i):
            start_to(*wide_piece(kind, (head + far_first(i, TP)) % TP))

    wide_start(0)

    pltpu.make_async_copy(len_in, len_ref, loc_s.at[0]).wait()
    pltpu.make_async_copy(grp_in, grp_ref, loc_s.at[1]).wait()
    lens = [len_ref[d] for d in range(NDOC)]
    first = [1 - grp_ref[d] for d in range(NDOC)]
    starts = []
    total = jnp.int32(0)
    for d in range(NDOC):
        starts.append(total)
        total = total + lens[d]

    def count0(position):
        acc = 0
        for d in range(NDOC):
            acc = acc + first[d] * jnp.minimum(jnp.maximum(position - starts[d], 0), lens[d])
        return acc

    sbase = here * (2 * BLK)
    base = sbase + half * BLK
    jl = lane_iota(REP * BLK)
    tok = base + (jl & (BLK - 1))
    low = jnp.zeros_like(tok)
    for d in range(NDOC):
        low = jnp.maximum(low, jnp.where(tok >= starts[d], starts[d], 0))
    low_ref[...] = low - sbase

    def slot(tok, begin, size):
        r0 = count0(begin)
        c0 = (count0(begin + size) - r0 + 15) >> 4
        before = count0(tok)
        is0 = count0(tok + 1) - before == 1
        rank = jnp.where(is0, before, tok - before)
        k = jnp.where(is0, (rank - r0) >> 4, c0 + ((rank - begin + r0) >> 4))
        return rank & (ZN - 1), k

    zd, k = slot(tok, base, BLK)
    code_z[...] = jnp.where(k < 8, zd * ZR + k * REP + (jl >> 7), -1)
    code_e[...] = jnp.where(k < 8, -REP - 1, zd * ZK + EXTRA + (jl >> 7))
    zd, k = slot(sbase + lane_iota(2 * BLK), sbase, 2 * BLK)
    code_zk[...] = zd * ZK + k

    row0 = count0(xi * (ZN * BLK))
    row1 = xi * (ZN * BLK) - row0

    def arrived(number, size, k):
        begin = xi * (ZN * BLK) + number * size
        r0 = count0(begin)
        r0e = count0(begin + size)
        r1 = begin - r0
        r1e = begin + size - r0e
        c0 = (r0e - r0 + 15) >> 4
        g0 = k < c0
        kk = jnp.where(g0, k, k - c0)
        rb = jnp.where(g0, r0, r1)
        re = jnp.where(g0, r0e, r1e)
        rank = rb + ((zi - rb) & (ZN - 1)) + ZN * kk
        xd = jnp.where(g0, 0, 2) + ((rank >> 4) & 1)
        q = (rank - jnp.where(g0, row0, row1)) >> 5
        return rank < re, xd, q

    jx = lane_iota(ZN * ZR)
    ok, xd, q = arrived(jx >> 5, BLK, (jx & (ZR - 1)) >> 2)
    code_x[...] = jnp.where(ok, xd * 256 + (jx & 3) * 64 + q, -1)
    jk = lane_iota(ZN * ZK)
    ok, xd, q = arrived(jk >> 6, 2 * BLK, jk & (ZK - 1))
    in_pair = jnp.where(ok, xd * 192 + ((jk >> 5) & 1) * 64 + q, -1)
    row = jk & (ZK - 1)
    begin = xi * (ZN * BLK) + (jk >> 5) * BLK
    holder = 0
    for d in range(1, NDOC):
        holder = holder + jnp.where(starts[d] <= begin, 1, 0)
    ok, xd, _ = arrived(jk >> 5, BLK, jnp.full_like(jk, 8))
    ninth = jnp.where(ok & (row < EXTRA + 8), xd * 192 + 128 + holder * 8 + row - EXTRA, -1)
    code_xk[...] = jnp.where(row < EXTRA, in_pair, ninth)

    jf = lane_iota(4 * 64)
    xs = jf >> 6
    g1 = xi // 2
    res = (xi % 2) * ZN + zi
    rs0 = count0(xs * (ZN * BLK))
    rs0e = count0((xs + 1) * (ZN * BLK))
    rsb = jnp.where(g1 == 1, xs * (ZN * BLK) - rs0, rs0)
    rse = jnp.where(g1 == 1, (xs + 1) * (ZN * BLK) - rs0e, rs0e)
    rank = rsb + ((res - rsb) & 31) + 32 * (jf & 63)
    code = jnp.where(rank < rse, rank >> 5, -1)
    bfin[...] = jnp.where(
        lax.broadcasted_iota(jnp.int32, (BLK, 256), 0) == code, 1.0, 0.0
    ).astype(BF16)

    xs = jf >> 6
    holder = (jf >> 3) & 7
    this_start = 0
    next_start = 0
    for d in range(NDOC - 1):
        this_start = this_start + jnp.where(holder == d, starts[d], 0)
        next_start = next_start + jnp.where(holder == d, starts[d + 1], 0)
    begin = ((next_start - 1) >> 7) << 7
    r0 = count0(begin)
    r0e = count0(begin + BLK)
    rank = begin - r0
    rank = rank + ((zi - rank) & (ZN - 1)) + ZN * (8 - ((r0e - r0 + 15) >> 4))
    ok = (holder < NDOC - 1) & (this_start <= begin) & ((begin >> 11) == xs)
    ok = ok & (rank < begin + BLK - r0e) & (2 + ((rank >> 4) & 1) == xi)
    code_f[...] = jnp.where(ok, rank >> 5, -1)

    def onehot(dst, code, rows, step, shift=0):
        begin = pl.multiple_of(step * rows, rows)
        ids = begin - shift + lax.broadcasted_iota(jnp.int32, (rows, dst.shape[1]), 0)
        dst[pl.ds(begin, rows), :] = jnp.where(ids == code[...], 1.0, 0.0).astype(BF16)

    @pl.loop(0, SUPS)
    def _(step):
        onehot(az, code_z, 64, step)
        onehot(aze.at[0], code_e, 64, step)
        onehot(aze.at[1], code_e, 64, step, REP)
        onehot(ax, code_x, 128, step)
        onehot(azk, code_zk, 64, step)
        onehot(axk, code_xk, 96, step)

    @pl.loop(0, TP)
    def _(i):
        for core in range(2):
            landed(kv.at[half, 0, rows16(core * BLK + i * 16), :], kv_rs.at[core, i])

    def gather(r):
        return copy_to(kv.at[half, 0], kv.at[half, r], ag_ss.at[r], ag_rs.at[r], ahead(r))

    def across(r):
        return copy_to(kv.at[half, r], kv.at[half, r], d_ss.at[r], d_rs.at[r], (c, twin))

    def take(r):
        landed(kv.at[half, r], ag_rs.at[r])
        across(r).start()

    def crossing_last(t):
        return jnp.where(t < SUPS // 2, 2 * t + 2, 2 * t + 1 - SUPS)

    @pl.loop(1, SUPS + 1)
    def _(r):
        gather(r).start()

    across(0).start()
    wide_start(1)

    def wide_landed(kind):
        @pl.loop(0, TP)
        def _(i):
            landed((qin, gin)[kind].at[rows16(i * 16), :], a_rs.at[kind, i])

    wide_landed(0)
    for h in range(REP):
        qs[h * BLK : (h + 1) * BLK, :] = qin[:, h * HD : (h + 1) * HD]

    heads = [slice(h * BLK, (h + 1) * BLK) for h in range(REP)]
    pairs = [slice(h * BLK, (h + 2) * BLK) for h in range(0, REP, 2)]
    m_ref[...] = jnp.full_like(m_ref, NEG)
    l_ref[...] = jnp.zeros_like(l_ref)
    ot[...] = jnp.zeros_like(ot)

    def scores(r, hs):
        raw = mm(kv[0, r], qs[hs, :], NT) * SCALE2
        place_in = lax.broadcasted_iota(jnp.int32, raw.shape, 0)
        if not isinstance(r, int):
            return jnp.where(place_in >= low_ref[:, hs] + 2 * BLK * r, raw, NEG)
        query = (lax.broadcasted_iota(jnp.int32, raw.shape, 1) & (BLK - 1)) + half * BLK
        return jnp.where((place_in <= query) & (place_in >= low_ref[:, hs]), raw, NEG)

    def forward(r):
        for hs in pairs:
            s2 = scores(r, hs)
            m_old = m_ref[:, hs]
            m = jnp.maximum(m_old, jnp.max(s2, axis=0, keepdims=True))
            p = jnp.exp2(s2 - m)
            fade = jnp.exp2(m_old - m)
            m_ref[:, hs] = m
            l_ref[:, hs] = l_ref[:, hs] * fade + jnp.sum(p, axis=0, keepdims=True)
            ot[:, hs] = ot[:, hs] * fade + mm(kv[1, r], p.astype(BF16), TN)

    landed(kv.at[1 - half, 0], d_rs.at[0])
    forward(0)
    take(crossing_last(0))

    @pl.loop(0, SUPS)
    def _(t):
        @pl.when(t < SUPS - 1)
        def _():
            take(crossing_last(t + 1))

        r = crossing_last(t)
        landed(kv.at[1 - half, r], d_rs.at[r])
        forward(r)

    wide_landed(1)
    for h, hs in enumerate(heads):
        grad = gin[:, h * HD : (h + 1) * HD]
        gs[hs, :] = grad
        mass = l_ref[:, hs]
        att = (ot[:, hs] / mass).astype(BF16)
        obf[:, hs] = att
        d_ref[:, hs] = jnp.sum(att.astype(F32) * grad.astype(F32).T, axis=0, keepdims=True)
        m_ref[:, hs] = m_ref[:, hs] + jnp.log2(mass)

    zbuf = ((zsend.at[0], zrecv.at[0]), (zsend.at[1], zrecv.at[1]), (zsend_k, zrecv_k))
    xbuf = ((xsend.at[0], xrecv.at[0]), (xsend.at[1], xrecv.at[1]), (xsend_k, xrecv_k))

    def z_move(kind, dst_z):
        send, recv = zbuf[kind]
        return (
            send.at[dst_z],
            recv.at[row_block],
            z_ss.at[kind, dst_z],
            z_rs.at[kind, row_block],
            (xi * ZN + dst_z, head),
        )

    def x_move(kind, dst_x):
        send, recv = xbuf[kind]
        return (
            send.at[dst_x],
            recv.at[:, xi],
            x_ss.at[kind, dst_x],
            x_rs.at[kind, xi],
            (dst_x * ZN + zi, me),
        )

    def z_start(kind):
        @pl.loop(0, ZN)
        def _(i):
            start_to(*z_move(kind, (zi + far_first(i, ZN)) % ZN))

    def z_wait(kind):
        @pl.loop(0, ZN)
        def _(i):
            landed(zbuf[kind][1].at[i], z_rs.at[kind, i])

    def x_start(kind):
        @pl.loop(0, XN)
        def _(i):
            start_to(*x_move(kind, (xi + far_first(i, XN)) % XN))

    def x_wait(kind):
        @pl.loop(0, XN)
        def _(i):
            landed(xbuf[kind][1].at[:, i], x_rs.at[kind, i])

    def z_left(kind):
        @pl.loop(0, ZN)
        def _(i):
            left(*z_move(kind, i))

    def x_left(kind):
        @pl.loop(0, XN)
        def _(i):
            left(*x_move(kind, i))

    def z_fill(kind, src):
        zsend[kind] = mm(az[...], src[...], NT).astype(BF16).reshape(ZN, ZR, HD)
        z_start(kind)
        extra[kind] = mm(aze[kind], src[...], NT)

    def x_fill(kind):
        z_wait(kind)
        rows = zrecv[kind].reshape(ZN * ZR, HD)
        xsend[kind] = mm(ax[...], rows, NN).astype(BF16).reshape(XN, REP, 64, HD)
        x_start(kind)

    def to_twin(r):
        return copy_to(part.at[r], got.at[r], p_ss.at[r], p_rs.at[r], (c, twin))

    def to_owner(r):
        return copy_to(rs_send.at[r], rs_recv.at[r], rs_ss.at[r], rs_rs.at[r], ahead(-r))

    def both_cores(r):
        landed(got.at[r], p_rs.at[r])
        return keep[r] + got[r].astype(F32)

    dqt[...] = jnp.zeros_like(dqt)
    z_fill(0, obf)

    def terms_of(r):
        dk = jnp.zeros((2 * BLK, HD), F32)
        dv = jnp.zeros((2 * BLK, HD), F32)
        for hs in pairs:
            p = jnp.exp2(scores(r, hs) - m_ref[:, hs])
            dv = dv + mm(p.astype(BF16), gs[hs, :], NN)
            dp = mm(kv[1, r], gs[hs, :], NT)
            ds = (p * (dp - d_ref[:, hs])).astype(BF16)
            dk = dk + mm(ds, qs[hs, :], NN)
            dqt[:, hs] += mm(kv[0, r], ds, TN)
        keep[r] = jnp.where(half == 0, dk, dv)
        part[r] = jnp.where(half == 0, dv, dk).astype(BF16)
        to_twin(r).start()

    def pass_on(r):
        rs_send[r] = both_cores(r).astype(BF16)
        to_owner(r).start()

    @pl.loop(1, SUPS + 1)
    def _(r):
        terms_of(r)

        @pl.when(r > 1)
        def _():
            pass_on(r - 1)

    terms_of(0)
    pass_on(SUPS)
    dqbf[...] = (dqt[...] * SCALE).astype(BF16)
    z_fill(1, dqbf)
    x_fill(0)
    terms = both_cores(0)
    for r in range(1, SUPS + 1):
        landed(rs_recv.at[r], rs_rs.at[r])
        terms = terms + rs_recv[r].astype(F32)
    rows = (terms * jnp.where(half == 0, SCALE, 1.0)).astype(BF16)
    last = mm(azk[...], rows, NN) + extra[0] + extra[1]
    zsend_k[...] = last.astype(BF16).reshape(ZN, ZK, HD)
    z_start(2)
    x_fill(1)

    @pl.loop(0, TP)
    def _(i):
        for kind in range(2):
            left(*wide_piece(kind, i))
            left(*kv_piece(kind, i))

    @pl.loop(1, SUPS + 1)
    def _(r):
        gather(r).wait_send()
        across(r).wait_send()
        to_twin(r).wait_send()
        to_owner(r).wait_send()

    across(0).wait_send()
    to_twin(0).wait_send()
    z_left(0)
    z_left(1)
    x_left(0)
    z_wait(2)
    rows = zrecv_k[...].reshape(ZN * ZK, HD)
    xsend_k[...] = mm(axk[...], rows, NN).astype(BF16).reshape(XN, PLANES, 64, HD)
    x_start(2)
    z_left(2)
    x_left(1)
    for kind in range(3):
        x_wait(kind)

    x_left(2)


def settle(
    rows_in, rows_k_in, place_in, code_in,
    o_out, dq_out, dk_out, dv_out,
    rows, rows_k, place, code, sems,
):
    loads = [
        pltpu.make_async_copy(src, dst, sems.at[i])
        for i, (src, dst) in enumerate(
            ((code_in, code), (place_in, place), (rows_k_in, rows_k), (rows_in, rows))
        )
    ]
    for load in loads:
        load.start()
    for load in loads:
        load.wait()
    late = rows_k[2].reshape(256, HD)
    lane = lax.broadcasted_iota(jnp.int32, (BLK, 256), 1) & 7
    found = lax.broadcasted_iota(jnp.int32, (BLK, 256), 0) == code[...]
    for kind, out in ((0, o_out), (1, dq_out)):
        for h in range(REP):
            pick = jnp.where(found & (lane == kind * REP + h), 1.0, 0.0).astype(BF16)
            both = mm(place[...], rows[kind, h].reshape(256, HD), NN) + mm(pick, late, NN)
            out[:, h * HD : (h + 1) * HD] = both.astype(BF16)
    dk_out[...] = mm(place[...], rows_k[0].reshape(256, HD), NN).astype(BF16)
    dv_out[...] = mm(place[...], rows_k[1].reshape(256, HD), NN).astype(BF16)


def body(queries, keys, values, out_grad, doc_lengths, doc_groups):
    anywhere = pl.BlockSpec(memory_space=pl.ANY)
    vmem = pl.BlockSpec(memory_space=pltpu.VMEM)
    wide = REP * HD
    dma = pltpu.SemaphoreType.DMA
    moved = pl.pallas_call(
        kernel,
        out_shape=(
            jax.ShapeDtypeStruct((2, REP, XN, 64, HD), BF16),
            jax.ShapeDtypeStruct((PLANES, XN, 64, HD), BF16),
            jax.ShapeDtypeStruct((BLK, 256), BF16),
            jax.ShapeDtypeStruct((1, 256), jnp.int32),
        ),
        in_specs=[anywhere] * 6,
        out_specs=(anywhere, anywhere, vmem, vmem),
        scratch_shapes=[
            pltpu.SMEM((NDOC,), jnp.int32),
            pltpu.SMEM((NDOC,), jnp.int32),
            pltpu.VMEM((BLK, wide), BF16),
            pltpu.VMEM((BLK, wide), BF16),
            pltpu.VMEM((2, SUPS + 1, 2 * BLK, HD), BF16),
            pltpu.VMEM((wide, HD), BF16),
            pltpu.VMEM((wide, HD), BF16),
            pltpu.VMEM((HD, wide), F32),
            pltpu.VMEM((HD, wide), BF16),
            pltpu.VMEM((1, wide), F32),
            pltpu.VMEM((1, wide), F32),
            pltpu.VMEM((1, wide), F32),
            pltpu.VMEM((HD, wide), F32),
            pltpu.VMEM((HD, wide), BF16),
            pltpu.VMEM((1, wide), jnp.int32),
            pltpu.VMEM((SUPS + 1, 2 * BLK, HD), F32),
            pltpu.VMEM((SUPS + 1, 2 * BLK, HD), BF16),
            pltpu.VMEM((SUPS + 1, 2 * BLK, HD), BF16),
            pltpu.VMEM((SUPS + 1, 2 * BLK, HD), BF16),
            pltpu.VMEM((SUPS + 1, 2 * BLK, HD), BF16),
            pltpu.VMEM((2, ZN, ZR, HD), BF16),
            pltpu.VMEM((2, ZN, ZR, HD), BF16),
            pltpu.VMEM((ZN, ZK, HD), BF16),
            pltpu.VMEM((ZN, ZK, HD), BF16),
            pltpu.VMEM((2, XN, REP, 64, HD), BF16),
            pltpu.VMEM((XN, PLANES, 64, HD), BF16),
            pltpu.VMEM((ZN * ZR, wide), BF16),
            pltpu.VMEM((XN * 256, ZN * ZR), BF16),
            pltpu.VMEM((ZN * ZK, 2 * BLK), BF16),
            pltpu.VMEM((XN * 64 * PLANES, ZN * ZK), BF16),
            pltpu.VMEM((2, ZN * ZK, wide), BF16),
            pltpu.VMEM((2, ZN * ZK, HD), F32),
            pltpu.VMEM((1, wide), jnp.int32),
            pltpu.VMEM((1, wide), jnp.int32),
            pltpu.VMEM((1, ZN * ZR), jnp.int32),
            pltpu.VMEM((1, 2 * BLK), jnp.int32),
            pltpu.VMEM((1, ZN * ZK), jnp.int32),
            dma((2, TP)),
            dma((2, TP)),
            dma((2, TP)),
            dma((2, TP)),
            dma((SUPS + 1,)),
            dma((SUPS + 1,)),
            dma((SUPS + 1,)),
            dma((SUPS + 1,)),
            dma((SUPS + 1,)),
            dma((SUPS + 1,)),
            dma((SUPS + 1,)),
            dma((SUPS + 1,)),
            dma((3, ZN)),
            dma((3, ZN)),
            dma((3, XN)),
            dma((3, XN)),
            dma((2,)),
        ],
        compiler_params=pltpu.CompilerParams(
            collective_id=0, has_side_effects=True, vmem_limit_bytes=60 * 1024 * 1024
        ),
    )(doc_lengths, doc_groups, queries, keys, values, out_grad)
    return pl.pallas_call(
        settle,
        out_shape=(
            jax.ShapeDtypeStruct((BLK, wide), BF16),
            jax.ShapeDtypeStruct((BLK, wide), BF16),
            jax.ShapeDtypeStruct((BLK, HD), BF16),
            jax.ShapeDtypeStruct((BLK, HD), BF16),
        ),
        in_specs=[anywhere] * 4,
        out_specs=(vmem,) * 4,
        scratch_shapes=[
            pltpu.VMEM((2, REP, XN, 64, HD), BF16),
            pltpu.VMEM((PLANES, XN, 64, HD), BF16),
            pltpu.VMEM((BLK, 256), BF16),
            pltpu.VMEM((1, 256), jnp.int32),
            dma((4,)),
        ],
        compiler_params=pltpu.CompilerParams(vmem_limit_bytes=60 * 1024 * 1024),
    )(*moved)


def solution(mesh):
    rows = P(("ctx", "tp"), None)
    in_specs = (rows, rows, rows, rows, P(), P())
    out_specs = (P("ctx", "tp"),) * 4
    return jax.shard_map(body, mesh=mesh, in_specs=in_specs, out_specs=out_specs, check_vma=False)
```
